256 devices in a mesh: lat: 16 (over x_hi, y, core), lon: 16 (over x_lo, z).
Axes of the slice: x: 4 (x_hi: 2, x_lo: 2; x = x_hi * 2 + x_lo), y: 4, z: 8, core: 2. Of those that a mesh axis runs over, the one named last changes fastest.
Arguments:
- series: bfloat16 [16, 16, 3, 64, 128, 128], P('lat', 'lon')
- station_count: int32 [16, 16], P('lat', 'lon'), may hold values from 32 to 128, as said below
- pair_count: int32 [16, 16], P('lat', 'lon'), may hold values from 64 to 256, as said below
- pair_list: int32 [16, 16, 3, 256], P('lat', 'lon'), may hold values from 0 to 8, as said below
- band_bins: int32 [16], replicated, may hold values from 1 to 63, as said below
Outputs:
- tensors: float32 [16, 16, 256, 12, 256], P('lat', 'lon')
The draws below stay inside these ranges and needn't reach their ends.
Inputs may be any that keep to these rules, and one draw needn't show every extreme that they name: `station_count`: slots below a tile's count hold live stations; some tile is full in every draw. `pair_count`: some tile's list is full in every draw; entries at and beyond a tile's count are ignored. `pair_list`: row 0 holds offset codes 0 to 8, rows 1 and 2 block numbers below 8. `band_bins`: 16 distinct bins; the lowest and the highest allowed bin are always among them.
All inputs are finite; a program needn't handle non-finite values.
Results may differ from the reference program's by a relative error of at most 0.00032.
Values may be sent and summed in bfloat16 or wider, within the bound.
A program may use at most 256 MiB of HBM per device.

```python
import math
import jax
import jax.numpy as jnp
from jax import lax

SLOTS = 128
BLOCK = 16
WIN = 64
LEN = 128
NBAND = 16
PAIRS_MAX = 256
N_LAT = 16
N_LON = 16


def draw_series(key, part):
    key = jax.random.fold_in(key, 1)
    key_source, key_couple, key_noise = jax.random.split(key, 3)
    source = jax.random.normal(key_source, (2, WIN, 1, LEN), jnp.float32)
    coupling = 0.5 * jax.random.normal(key_couple, (N_LAT, N_LON, 3, 2, 1, SLOTS, 1), jnp.float32)
    coupling = coupling + jnp.eye(3, 2, dtype=jnp.float32)[None, None, :, :, None, None, None]
    rows = jnp.arange(N_LAT, dtype=jnp.float32) / max(N_LAT - 1, 1)
    shape = (N_LAT, N_LON, 3, WIN, SLOTS, LEN)
    noise = 0.6 * jax.random.normal(key_noise, shape, jnp.float32)
    amplitude = 1.0 + 2.0 * rows
    field = coupling[:, :, :, 0] * source[0] + coupling[:, :, :, 1] * source[1] + noise
    field = field * amplitude[:, None, None, None, None, None]
    return field.astype(jnp.bfloat16)


def draw_station_count(key, part):
    key = jax.random.fold_in(key, 2)
    key_counts, key_full = jax.random.split(key)
    counts = jax.random.randint(key_counts, (N_LAT * N_LON,), SLOTS // 4, SLOTS + 1)
    full_tile = jax.random.randint(key_full, (), 0, N_LAT * N_LON)
    counts = counts.at[full_tile].set(SLOTS)
    return counts.reshape(N_LAT, N_LON).astype(jnp.int32)


def draw_pair_count(key, part):
    key = jax.random.fold_in(key, 3)
    key_counts, key_full = jax.random.split(key)
    steps = jax.random.randint(key_counts, (N_LAT * N_LON,), 0, 13)
    counts = PAIRS_MAX // 4 + PAIRS_MAX * 3 // 4 * steps * steps // 144
    full_tile = jax.random.randint(key_full, (), 0, N_LAT * N_LON)
    counts = counts.at[full_tile].set(PAIRS_MAX)
    return counts.reshape(N_LAT, N_LON).astype(jnp.int32)


def draw_pair_list(key, part):
    key = jax.random.fold_in(key, 4)
    key_offset, key_local, key_near = jax.random.split(key, 3)
    shape = (N_LAT, N_LON, PAIRS_MAX)
    offsets = jax.random.randint(key_offset, shape, 0, 9)
    local_blocks = jax.random.randint(key_local, shape, 0, SLOTS // BLOCK)
    near_blocks = jax.random.randint(key_near, shape, 0, SLOTS // BLOCK)
    return jnp.stack([offsets, local_blocks, near_blocks], axis=2).astype(jnp.int32)


def draw_band_bins(key, part):
    key = jax.random.fold_in(key, 5)
    key_inner, key_order = jax.random.split(key)
    inner = jax.random.permutation(key_inner, LEN // 2 - 3) + 2
    ends = jnp.array([1, LEN // 2 - 1], dtype=jnp.int32)
    chosen = jnp.concatenate([ends, inner[:NBAND - 2].astype(jnp.int32)])
    return jax.random.permutation(key_order, chosen).astype(jnp.int32)


def setup_inputs(seed: int = 0) -> dict:
    keys = jax.random.split(jax.random.key(seed), 6)
    series = draw_series(jax.random.fold_in(keys[5], 71), 0)
    station_count = draw_station_count(jax.random.fold_in(keys[5], 71), 0)
    pair_count = draw_pair_count(jax.random.fold_in(keys[5], 71), 0)
    pair_list = draw_pair_list(jax.random.fold_in(keys[5], 71), 0)
    band_bins = draw_band_bins(jax.random.fold_in(keys[5], 71), 0)
    return dict(series=series, station_count=station_count, pair_count=pair_count, pair_list=pair_list, band_bins=band_bins)


def dft_table(band_bins, length):
    samples = jnp.arange(length, dtype=jnp.int32)
    phase = band_bins.astype(jnp.int32)[None, :] * samples[:, None] % length
    angle = phase.astype(jnp.float32) * (2.0 * math.pi / length)
    factor = 1.0 / math.sqrt(length)
    table = jnp.stack([jnp.cos(angle) * factor, -jnp.sin(angle) * factor], axis=1)
    return table.astype(jnp.bfloat16)

def tile_spectra(series_tile, table, count):
    spectra = jnp.einsum('cwsn,nrk->csrkw', series_tile.astype(jnp.float32), table.astype(jnp.float32))
    comps, slots = (spectra.shape[0], spectra.shape[1])
    spectra = spectra.reshape(comps, slots, 2, -1)
    live = (jnp.arange(slots, dtype=jnp.int32) < count).astype(jnp.float32)
    spectra = (spectra * live[None, :, None, None]).astype(jnp.bfloat16)
    horizontal = spectra[:2].astype(jnp.float32)
    return (spectra, 0.5 * jnp.sum(horizontal * horizontal))

def gram_terms(nearby):
    real_x, imag_x = (nearby[:, 0, :, 0, :], nearby[:, 0, :, 1, :])
    real_y, imag_y = (nearby[:, 1, :, 0, :], nearby[:, 1, :, 1, :])
    gram_xx = lax.optimization_barrier(jnp.sum(real_x * real_x + imag_x * imag_x, -1))
    gram_yy = lax.optimization_barrier(jnp.sum(real_y * real_y + imag_y * imag_y, -1))
    gram_re = lax.optimization_barrier(jnp.sum(real_x * real_y + imag_x * imag_y, -1))
    gram_im = lax.optimization_barrier(jnp.sum(real_x * imag_y - imag_x * real_y, -1))
    return (gram_xx, gram_yy, gram_re, gram_im)

def solve_pair(cross_re, cross_im, gram_xx, gram_yy, gram_re, gram_im, ridge):
    upper_xx = gram_xx + ridge
    lower_yy = gram_yy + ridge
    determinant = upper_xx * lower_yy - (gram_re * gram_re + gram_im * gram_im)
    first_re, second_re = (cross_re[:, :, 0], cross_re[:, :, 1])
    first_im, second_im = (cross_im[:, :, 0], cross_im[:, :, 1])
    top_re = (lower_yy * first_re - (gram_re * second_re - gram_im * second_im)) / determinant
    top_im = (lower_yy * first_im - (gram_re * second_im + gram_im * second_re)) / determinant
    low_re = (upper_xx * second_re - (gram_re * first_re + gram_im * first_im)) / determinant
    low_im = (upper_xx * second_im - (gram_re * first_im - gram_im * first_re)) / determinant
    stacked = jnp.stack([jnp.stack([top_re, top_im], 1), jnp.stack([low_re, low_im], 1)], 0)
    block = stacked.shape[3]
    return stacked.reshape(12, block * block)

def tile_pairs(spectra, nearby_raw, listing, live_pairs, ridge, block):
    targets = spectra.astype(jnp.float32)
    nearby = nearby_raw.astype(jnp.float32)
    gram_xx, gram_yy, gram_re, gram_im = gram_terms(nearby)

    def pick(values, offset, start):
        chosen = lax.dynamic_index_in_dim(values, offset, 0, keepdims=False)
        return lax.dynamic_slice_in_dim(chosen, start, block, 0)

    def one_pair(record):
        offset = record[0].astype(jnp.int32)
        local_start = (record[1] * block).astype(jnp.int32)
        near_start = (record[2] * block).astype(jnp.int32)
        target = lax.dynamic_slice_in_dim(targets, local_start, block, 1)
        chosen = lax.dynamic_index_in_dim(nearby, offset, 0, keepdims=False)
        partner = lax.dynamic_slice_in_dim(chosen, near_start, block, 1)
        cross_re = jnp.einsum('tim,ajm->tiaj', target[:, :, 0], partner[:, :, 0]) + jnp.einsum('tim,ajm->tiaj', target[:, :, 1], partner[:, :, 1])
        cross_im = jnp.einsum('tim,ajm->tiaj', target[:, :, 1], partner[:, :, 0]) - jnp.einsum('tim,ajm->tiaj', target[:, :, 0], partner[:, :, 1])
        return solve_pair(cross_re, cross_im, pick(gram_xx, offset, near_start), pick(gram_yy, offset, near_start), pick(gram_re, offset, near_start), pick(gram_im, offset, near_start), ridge)
    solved = jax.vmap(one_pair)(listing.T)
    pairs = listing.shape[1]
    keep = (jnp.arange(pairs, dtype=jnp.int32) < live_pairs).astype(jnp.float32)
    return solved * keep[:, None, None]

def reference(series, station_count, pair_count, pair_list, band_bins):
    table = dft_table(band_bins, series.shape[-1])
    tiles = N_LAT * N_LON
    flat_series = series.reshape((tiles,) + series.shape[2:])
    flat_count = station_count.reshape(tiles)
    spectra, powers = lax.map(lambda record: tile_spectra(record[0], table, record[1]), (flat_series, flat_count))
    ridge = jnp.sum(powers) / jnp.sum(station_count.astype(jnp.float32)) + 1e-06
    slots, width = (spectra.shape[2], spectra.shape[4])
    grid = spectra[:, :2].reshape(N_LAT, N_LON, 2, slots, 2, width)
    padded = jnp.pad(grid, ((1, 1), (1, 1), (0, 0), (0, 0), (0, 0), (0, 0)))
    flat_lists = pair_list.reshape(tiles, 3, -1)
    flat_pairs = pair_count.reshape(tiles)
    zero = jnp.zeros((), jnp.int32)

    def one_tile(record):
        tile_index, tile_spec, listing, live_pairs = record
        tile_row = (tile_index // N_LON).astype(jnp.int32)
        tile_column = (tile_index % N_LON).astype(jnp.int32)
        nearby = lax.dynamic_slice(padded, (tile_row, tile_column, zero, zero, zero, zero), (3, 3, 2, slots, 2, width))
        nearby = nearby.reshape(9, 2, slots, 2, width)
        return tile_pairs(tile_spec, nearby, listing, live_pairs, ridge, BLOCK)
    result = lax.map(one_tile, (jnp.arange(tiles, dtype=jnp.int32), spectra, flat_lists, flat_pairs))
    return result.reshape((N_LAT, N_LON) + result.shape[1:])
```

```python
import functools
import math

import jax
import jax.numpy as jnp
import ml_dtypes
import numpy as np
from jax import lax
from jax.experimental import pallas as pl
from jax.experimental.pallas import tpu as pltpu
from jax.sharding import PartitionSpec as P

BLOCK = 16
SLOTS = 128
WIN = 64
LEN = 128
NBAND = 16
GROUPS = 8
BLOCKS = SLOTS // BLOCK
F32 = jnp.float32
BF16 = jnp.bfloat16


def dft_matrix():
    samples = np.arange(LEN)
    bins = np.arange(LEN // 2)
    phase = (samples[:, None] * bins[None]) % LEN
    angle = phase.astype(np.float32) * np.float32(2.0 * math.pi / LEN)
    factor = np.float32(1.0 / math.sqrt(LEN))
    both = np.concatenate([np.cos(angle) * factor, -np.sin(angle) * factor], axis=1)
    return both.astype(ml_dtypes.bfloat16)


def nt_dot(a, b):
    return lax.dot_general(a, b, (((1,), (1,)), ((), ())), preferred_element_type=F32)


def group_transpose(parts):
    lane = lax.broadcasted_iota(jnp.int32, parts[0].shape, 1)
    group = lane // BLOCK
    v = [x if i == 0 else pltpu.roll(x, i * BLOCK, 1) for i, x in enumerate(parts)]
    for bit in (1, 2, 4):
        mask = (group // bit) % 2 == 1
        v = [jnp.where(mask, v[(k + bit) % 8], v[k]) for k in range(8)]
    out = []
    for q in range(8):
        x = v[(-q) % 8]
        out.append(x if q == 0 else pltpu.roll(x, LEN - q * BLOCK, 1))
    return out


def kernel(
    n_lat, n_lon, dims,
    count_ref, pairs_ref, list_ref, bins_ref, dft_ref, series_ref, out_ref,
    xbuf, tab, own, near, lhs, gram, red_send, red_recv, cross, solved,
    series_sem, own_send, fwd_send, lon_recv, lat_recv,
    gown_send, gfwd_send, gram_recv, rsend, rrecv,
):
    lat, lon = lax.axis_index("lat"), lax.axis_index("lon")
    has_up, has_down = lat > 0, lat < n_lat - 1
    has_left, has_right = lon > 0, lon < n_lon - 1

    def dev(la, lo):
        return (la, lo)

    steps = []
    bit = 1
    while bit < n_lat:
        steps.append(("lat", bit))
        bit *= 2
    bit = 1
    while bit < n_lon:
        steps.append(("lon", bit))
        bit *= 2

    def partner(step):
        axis, b = step
        if axis == "lat":
            return dev(lat + b * (1 - 2 * ((lat // b) % 2)), lon)
        return dev(lat, lon + b * (1 - 2 * ((lon // b) % 2)))

    sides = (
        (has_up, dev(lat - 1, lon)),
        (has_down, dev(lat + 1, lon)),
        (has_left, dev(lat, lon - 1)),
        (has_right, dev(lat, lon + 1)),
    )
    MESH = pl.DeviceIdType.MESH
    barrier = pltpu.get_barrier_semaphore()
    for here, target in sides:
        @pl.when(here)
        def _(target=target):
            pl.semaphore_signal(barrier, inc=1, device_id=target, device_id_type=MESH)
    for step in steps:
        pl.semaphore_signal(barrier, inc=1, device_id=partner(step), device_id_type=MESH)

    def series_copy(g):
        return pltpu.make_async_copy(
            series_ref.at[:, pl.ds(g * 8, 8)], xbuf.at[:, pl.ds(g * 8, 8)], series_sem.at[g]
        )

    for g in range(GROUPS):
        series_copy(g).start()

    lane = lax.broadcasted_iota(jnp.int32, (LEN, 256), 1)
    row = lax.broadcasted_iota(jnp.int32, (LEN, 256), 0)
    bins = jnp.zeros((LEN, 256), jnp.int32)
    for k in range(NBAND):
        bins = jnp.where(lane % NBAND == k, bins_ref[k], bins)
    chosen = (row % 64 == bins) & (row // 64 == lane // 128)
    full = jnp.dot(dft_ref[...], chosen.astype(F32).astype(BF16), preferred_element_type=F32)
    window = (lane // NBAND) % 8
    for j in range(4):
        for h in range(2):
            tab[j, h * LEN:(h + 1) * LEN, :] = jnp.where(window == 2 * j + h, full, 0.0).astype(BF16)
    prow = lax.broadcasted_iota(jnp.int32, (SLOTS, SLOTS), 0)
    pcol = lax.broadcasted_iota(jnp.int32, (SLOTS, SLOTS), 1)
    diagonal = pcol == (prow % BLOCKS) * BLOCK + prow // BLOCKS
    permute = diagonal.astype(F32).astype(BF16)
    live = row < count_ref[0, 0]

    def clear(o):
        near[o] = jnp.zeros(near.shape[1:], BF16)
        gram[o] = jnp.zeros(gram.shape[1:], F32)

    for o in range(9):
        di, dj = o // 3 - 1, o % 3 - 1
        if o == 4:
            continue
        inside = (lat + di >= 0) & (lat + di < n_lat) & (lon + dj >= 0) & (lon + dj < n_lon)

        @pl.when(jnp.logical_not(inside))
        def _(o=o):
            clear(o)

    here_count = (
        has_up.astype(jnp.int32) + has_down.astype(jnp.int32)
        + has_left.astype(jnp.int32) + has_right.astype(jnp.int32)
    )
    pl.semaphore_wait(barrier, here_count + len(steps))

    slots = (7, 1, 5, 3)

    def own_copy(side, g):
        piece = own if g is None else own.at[g]
        slot = near.at[slots[side]] if g is None else near.at[slots[side], g]
        sem = lon_recv.at[side - 2, 0 if g is None else g] if side >= 2 else lat_recv.at[slots[side]]
        return pltpu.make_async_remote_copy(
            src_ref=piece, dst_ref=slot, send_sem=own_send.at[side], recv_sem=sem,
            device_id=sides[side][1], device_id_type=MESH,
        )

    def spectra_step(g, _):
        series_copy(g).wait()
        for c in range(3):
            total = None
            for j in range(4):
                x = jnp.concatenate([xbuf[c, g * 8 + 2 * j], xbuf[c, g * 8 + 2 * j + 1]], axis=1)
                part = jnp.dot(x, tab[j], preferred_element_type=F32)
                total = part if total is None else total + part
            spec = jnp.where(live, total, 0.0).astype(BF16)
            if c < 2:
                own[g, c * SLOTS:(c + 1) * SLOTS, :] = spec
            mixed = jnp.dot(permute, spec, preferred_element_type=F32).astype(BF16)
            lhs[g, c * SLOTS:(c + 1) * SLOTS, :] = mixed
            lhs[g, 384 + c * SLOTS:384 + (c + 1) * SLOTS, 0:128] = mixed[:, 128:256]
            lhs[g, 384 + c * SLOTS:384 + (c + 1) * SLOTS, 128:256] = -mixed[:, 0:128]
        for side in range(4):
            @pl.when(sides[side][0])
            def _(side=side):
                own_copy(side, g).start()
        return 0

    lax.fori_loop(0, GROUPS, spectra_step, 0)

    def cross_block(source):
        for m in range(3):
            total = None
            for g in range(GROUPS):
                part = nt_dot(lhs[g, m * 256:(m + 1) * 256, :], source(g))
                total = part if total is None else total + part
            cross[m * 256:(m + 1) * 256, :] = total

    def pick(r, t, a):
        block = cross[r * 384 + t * 128:r * 384 + (t + 1) * 128, a * 128:(a + 1) * 128]
        return jnp.sum(jnp.where(diagonal, block, 0.0), axis=0, keepdims=True)

    cross_block(lambda g: own[g])
    gxx, gyy, gre, gim = pick(0, 0, 0), pick(0, 1, 1), pick(0, 1, 0), pick(1, 1, 0)
    gram[4] = jnp.concatenate([gxx, gyy, gre, gim, gxx, gyy, gre, gim], axis=0)
    power = 0.5 * jnp.sum(gxx + gyy, axis=1, keepdims=True)
    srow = lax.broadcasted_iota(jnp.int32, (8, 128), 0)
    count = count_ref[0, 0].astype(F32)
    red_send[0] = jnp.where(srow == 0, jnp.broadcast_to(power, (8, 128)), count)

    def gram_copy(side):
        return pltpu.make_async_remote_copy(
            src_ref=gram.at[4], dst_ref=gram.at[slots[side]], send_sem=gown_send.at[side],
            recv_sem=gram_recv.at[slots[side]], device_id=sides[side][1], device_id_type=MESH,
        )

    for side in range(4):
        @pl.when(sides[side][0])
        def _(side=side):
            gram_copy(side).start()

    forwards = ((3, 0, 6), (3, 1, 0), (5, 0, 8), (5, 1, 2))

    def fwd_copy(f, g):
        source, side, slot = forwards[f]
        return pltpu.make_async_remote_copy(
            src_ref=near.at[source] if g is None else near.at[source, g],
            dst_ref=near.at[slot] if g is None else near.at[slot, g],
            send_sem=fwd_send.at[f], recv_sem=lat_recv.at[slot],
            device_id=sides[side][1], device_id_type=MESH,
        )

    def fwd_gram(f):
        source, side, slot = forwards[f]
        return pltpu.make_async_remote_copy(
            src_ref=gram.at[source], dst_ref=gram.at[slot], send_sem=gfwd_send.at[f],
            recv_sem=gram_recv.at[slot], device_id=sides[side][1], device_id_type=MESH,
        )

    def each_forward(action):
        for f, (source, side, _) in enumerate(forwards):
            has_source = has_left if source == 3 else has_right

            @pl.when(has_source & sides[side][0])
            def _(f=f):
                action(f)

    arrivals = ((3, has_left, 1), (5, has_right, 0))

    def lon_wait(slot, index, g):
        pltpu.make_async_remote_copy(
            src_ref=near.at[slot, g], dst_ref=near.at[slot, g], send_sem=own_send.at[0],
            recv_sem=lon_recv.at[index, g], device_id=sides[0][1], device_id_type=MESH,
        ).wait_recv()

    def gram_wait(slot):
        pltpu.make_async_remote_copy(
            src_ref=gram.at[slot], dst_ref=gram.at[slot], send_sem=gown_send.at[0],
            recv_sem=gram_recv.at[slot], device_id=sides[0][1], device_id_type=MESH,
        ).wait_recv()

    def reduce_start(s):
        pltpu.make_async_remote_copy(
            src_ref=red_send.at[s], dst_ref=red_recv.at[s], send_sem=rsend.at[s], recv_sem=rrecv.at[s],
            device_id=partner(steps[s]), device_id_type=MESH,
        ).start()

    def reduce_end(s):
        pltpu.make_async_remote_copy(
            src_ref=red_send.at[s], dst_ref=red_recv.at[s], send_sem=rsend.at[s], recv_sem=rrecv.at[s],
            device_id=partner(steps[s]), device_id_type=MESH,
        ).wait()
        red_send[s + 1] = red_send[s] + red_recv[s]

    for slot, here, _ in arrivals:
        @pl.when(here)
        def _(slot=slot):
            gram_wait(slot)
    each_forward(lambda f: fwd_gram(f).start())

    for g in range(GROUPS):
        if g < len(steps):
            reduce_start(g)
        for slot, here, index in arrivals:
            @pl.when(here)
            def _(slot=slot, index=index, g=g):
                lon_wait(slot, index, g)
            for f, (source, side, _) in enumerate(forwards):
                if source == slot:
                    @pl.when(here & sides[side][0])
                    def _(f=f, g=g):
                        fwd_copy(f, g).start()
        if g < len(steps):
            reduce_end(g)

    total = red_send[len(steps)]
    ridge = total[0:1, :] / total[1:2, :] + 1e-06

    def solve_tile(o):
        terms = gram[o]
        upper = terms[0:1] + ridge
        lower = terms[1:2] + ridge
        gre, gim = terms[2:3], terms[3:4]
        inverse = 1.0 / (upper * lower - (gre * gre + gim * gim))
        wide = lambda v: jnp.broadcast_to(v * inverse, (8, 128))
        upper, lower, gre, gim = wide(upper), wide(lower), wide(gre), wide(gim)
        for t in range(3):
            for half in range(2):
                parts = [[], [], [], []]
                for i in range(8):
                    base = t * 128 + (half * 8 + i) * 8
                    first_re = cross[base:base + 8, 0:128]
                    second_re = cross[base:base + 8, 128:256]
                    first_im = cross[384 + base:384 + base + 8, 0:128]
                    second_im = cross[384 + base:384 + base + 8, 128:256]
                    parts[0].append(lower * first_re - (gre * second_re - gim * second_im))
                    parts[1].append(lower * first_im - (gre * second_im + gim * second_re))
                    parts[2].append(upper * second_re - (gre * first_re + gim * first_im))
                    parts[3].append(upper * second_im - (gre * first_im - gim * first_re))
                for ar in range(4):
                    plane = ((ar // 2) * 3 + t) * 2 + ar % 2
                    moved = group_transpose(parts[ar])
                    for q in range(8):
                        solved[plane, pl.ds(o * 64 + q * 8, 8), half * 128:(half + 1) * 128] = moved[q]

    solve_own = lambda: solve_tile(4)
    solve_own()

    even = lat % 2 == 0
    fast = jnp.where(even, 2, 0)
    slow = 2 - fast

    def tile_step(k, _):
        is_slow = (k == 3) | (k >= 6)
        di = jnp.where(k < 2, 1, jnp.where(is_slow, slow, fast))
        dj = jnp.where(k < 2, 2 * k, jnp.where(k < 4, 1, 2 * (k % 2)))
        o = di * 3 + dj
        la, lo = lat + di - 1, lon + dj - 1
        inside = (la >= 0) & (la < n_lat) & (lo >= 0) & (lo < n_lon)

        @pl.when(inside & (k >= 2))
        def _():
            pltpu.make_async_remote_copy(
                src_ref=near.at[o], dst_ref=near.at[o], send_sem=own_send.at[0],
                recv_sem=lat_recv.at[o], device_id=sides[0][1], device_id_type=MESH,
            ).wait_recv()
            gram_wait(o)
        cross_block(lambda g: near[o, g])
        solve_tile(o)
        return 0

    lax.fori_loop(0, 8, tile_step, 0)

    for plane in range(12):
        solved[plane, 576:584, :] = jnp.zeros((8, 256), F32)
    live_pairs = pairs_ref[0, 0]

    def gather_step(e, _):
        source = list_ref[0, e] * 64 + list_ref[2, e] * 8 + list_ref[1, e]
        source = jnp.where(e < live_pairs, source, 576)
        for plane in range(12):
            out_ref[plane, pl.ds(e, 1), :] = solved[plane, pl.ds(source, 1), :]
        return 0

    lax.fori_loop(0, dims[0], gather_step, 0)

    for side in range(4):
        @pl.when(sides[side][0])
        def _(side=side):
            own_copy(side, None).wait_send()
            gram_copy(side).wait_send()

    def finish(f):
        fwd_copy(f, None).wait_send()
        fwd_gram(f).wait_send()

    each_forward(finish)


def per_device(n_lat, n_lon, series, station_count, pair_count, pair_list, band_bins):
    pairs = pair_list.shape[-1]
    smem = pl.BlockSpec(memory_space=pltpu.SMEM)
    vmem = pl.BlockSpec(memory_space=pltpu.VMEM)
    steps = (n_lat - 1).bit_length() + (n_lon - 1).bit_length()
    dma = pltpu.SemaphoreType.DMA
    solved = pl.pallas_call(
        functools.partial(kernel, n_lat, n_lon, (pairs,)),
        out_shape=jax.ShapeDtypeStruct((12, pairs, BLOCK * BLOCK), F32),
        in_specs=[smem, smem, smem, smem, vmem, pl.BlockSpec(memory_space=pl.ANY)],
        out_specs=vmem,
        scratch_shapes=[
            pltpu.VMEM((3, WIN, SLOTS, LEN), BF16),
            pltpu.VMEM((4, 2 * LEN, 256), BF16),
            pltpu.VMEM((GROUPS, 256, 256), BF16),
            pltpu.VMEM((9, GROUPS, 256, 256), BF16),
            pltpu.VMEM((GROUPS, 768, 256), BF16),
            pltpu.VMEM((9, 8, 128), F32),
            pltpu.VMEM((steps + 1, 8, 128), F32),
            pltpu.VMEM((steps, 8, 128), F32),
            pltpu.VMEM((768, 256), F32),
            pltpu.VMEM((12, 584, 256), F32),
            dma((GROUPS,)),
            dma((4,)),
            dma((4,)),
            dma((2, GROUPS)),
            dma((9,)),
            dma((4,)),
            dma((4,)),
            dma((9,)),
            dma((steps,)),
            dma((steps,)),
        ],
        compiler_params=pltpu.CompilerParams(
            collective_id=0, has_side_effects=True, vmem_limit_bytes=56 * 1024 * 1024
        ),
    )(
        station_count,
        pair_count,
        pair_list.reshape(3, pairs),
        band_bins,
        jnp.asarray(dft_matrix()),
        series.reshape(3, WIN, SLOTS, LEN),
    )
    return solved.transpose(1, 0, 2)[None, None]


def solution(mesh):
    in_specs = (
        P("lat", "lon", None, None, None, None),
        P("lat", "lon"),
        P("lat", "lon"),
        P("lat", "lon", None, None),
        P(),
    )
    out_specs = P("lat", "lon", None, None, None)
    return jax.shard_map(
        functools.partial(per_device, mesh.shape["lat"], mesh.shape["lon"]),
        mesh=mesh, in_specs=in_specs, out_specs=out_specs, check_vma=False,
    )
```

```python
import functools
import math

import jax
import jax.numpy as jnp
import ml_dtypes
import numpy as np
from jax import lax
from jax.experimental import pallas as pl
from jax.experimental.pallas import tpu as pltpu
from jax.sharding import PartitionSpec as P

BLOCK = 16
SLOTS = 128
WIN = 64
LEN = 128
NBAND = 16
GROUPS = 8
FIRST = 1
AHEAD = 2
EARLY = 0
F32 = jnp.float32
BF16 = jnp.bfloat16
MESH = pl.DeviceIdType.MESH

LEFT, RIGHT, FAST, SLOW, FAST_LEFT, FAST_RIGHT, SLOW_LEFT, SLOW_RIGHT, OWN = range(9)


def dft_matrix():
    samples = np.arange(LEN)
    bins = np.arange(LEN // 2)
    phase = (samples[:, None] * bins[None]) % LEN
    angle = phase.astype(np.float32) * np.float32(2.0 * math.pi / LEN)
    factor = np.float32(1.0 / math.sqrt(LEN))
    both = np.concatenate([np.cos(angle) * factor, -np.sin(angle) * factor], axis=1)
    return both.astype(ml_dtypes.bfloat16)


def nt_dot(a, b):
    return lax.dot_general(a, b, (((1,), (1,)), ((), ())), preferred_element_type=F32)


def group_transpose(parts, masks):
    def skew(v):
        for bit, mask in zip((1, 2, 4), masks):
            v = [jnp.where(mask, v[(k + bit) % 8], v[k]) for k in range(8)]
        return v

    v = [x if d == 0 else pltpu.roll(x, d * BLOCK, 1) for d, x in enumerate(skew(parts))]
    v = skew(v)
    return [v[(-q) % 8] for q in range(8)]


def kernel(
    n_lat, n_lon, pairs,
    count_ref, pairs_ref, bins_ref, list_ref, dft_ref, series_ref, out_ref,
    xbuf, tab, near, lhs, gram, power_ref, red_send, red_recv, a_recv, z_recv, cross, picked, code_ref, coef_ref,
    series_sem, near_recv, own_send, fwd_send, gram_recv, gown_send, gfwd_send, rsend, rrecv, a_send_sem, a_recv_sem, z_send_sem, z_recv_sem,
):
    lat, lon = lax.axis_index("lat"), lax.axis_index("lon")
    parity = lat % 2
    fast_lat = lat + 1 - 2 * parity
    slow_lat = lat - 1 + 2 * parity
    has_slow = (slow_lat >= 0) & (slow_lat < n_lat)
    has_left, has_right = lon > 0, lon < n_lon - 1
    middle = (lat == n_lat // 2 - 1) | (lat == n_lat // 2)
    special = middle & ((lon == 0) | (lon == n_lon - 1))
    left_special = middle & (lon == 1)
    right_special = middle & (lon == n_lon - 2)

    left_dev, right_dev = (lat, lon - 1), (lat, lon + 1)
    fast_dev, slow_dev = (fast_lat, lon), (slow_lat, lon)
    sides = {LEFT: (has_left, left_dev), RIGHT: (has_right, right_dev),
             FAST: (None, fast_dev), SLOW: (has_slow, slow_dev)}
    lands = {LEFT: RIGHT, RIGHT: LEFT, FAST: FAST, SLOW: SLOW}

    def when(cond, action):
        if cond is None:
            action()
        else:
            pl.when(cond)(action)

    def both(*conds):
        conds = [c for c in conds if c is not None]
        total = None
        for c in conds:
            total = c if total is None else total & c
        return total

    half_lat, half_lon = n_lat // 2, n_lon // 2
    ys, zs = half_lat // 2, half_lon
    x_hi, y = lat // half_lat, lat % half_lat // 2
    x_lo, z = lon // half_lon, lon % half_lon

    def across(d):
        x = (2 * x_hi + x_lo + d % 4) % 4
        return (x // 2 * half_lat + y * 2 + (parity + d // 4) % 2, x % 2 * half_lon + z)

    def along_z(d):
        return (lat, x_lo * half_lon + (z + d) % zs)

    def along_y(d):
        return (x_hi * half_lat + (y + d + ys) % ys * 2 + parity, lon)

    stages = [((1, -1) if k < (ys - 1) // 2 else (1,), k > 0) for k in range(ys // 2)]
    rings = [along_y(d) for d in ((1, -1) if ys > 1 else ())]
    rings += [across(d) for d in range(1, 8)] + [along_z(d) for d in range(1, zs)]

    barrier = pltpu.get_barrier_semaphore()

    def greet(target):
        pl.semaphore_signal(barrier, inc=1, device_id=target, device_id_type=MESH)

    gram[...] = jnp.zeros((9, 8, 128), F32)
    for here, target in sides.values():
        when(here, functools.partial(greet, target))
    for target in rings:
        greet(target)

    def series_copy(g):
        return pltpu.make_async_copy(
            series_ref.at[:, pl.ds(g * 8, 8)], xbuf.at[:, pl.ds(g * 8, 8)], series_sem.at[g]
        )

    for g in range(GROUPS):
        series_copy(g).start()

    lane = lax.broadcasted_iota(jnp.int32, (LEN, 256), 1)
    row = lax.broadcasted_iota(jnp.int32, (LEN, 256), 0)
    bins = jnp.zeros((LEN, 256), jnp.int32)
    for k in range(NBAND):
        bins = jnp.where(lane % NBAND == k, bins_ref[k], bins)
    chosen = (row % 64 == bins) & (row // 64 == lane // 128)
    full = jnp.dot(dft_ref[...], chosen.astype(F32).astype(BF16), preferred_element_type=F32)
    window = (lane // NBAND) % 8
    for j in range(4):
        for h in range(2):
            tab[j, h * LEN:(h + 1) * LEN, :] = jnp.where(window == 2 * j + h, full, 0.0).astype(BF16)
    live = row < count_ref[0, 0]
    power_ref[...] = jnp.zeros((8, 256), F32)

    listing = list_ref[...].astype(F32)
    code = listing[0] * 64.0 + listing[2] * 8.0 + listing[1]
    entry = lax.broadcasted_iota(jnp.int32, (1, pairs), 1)
    code = jnp.where(entry < pairs_ref[0, 0], code, -1.0)
    code_ref[...] = jnp.broadcast_to(code, (128, pairs)).T

    greeted = (
        has_slow.astype(jnp.int32) + has_left.astype(jnp.int32) + has_right.astype(jnp.int32)
        + (1 + len(rings))
    )
    pl.semaphore_wait(barrier, greeted)

    def remote(src, dst, send, recv, device):
        return pltpu.make_async_remote_copy(
            src_ref=src, dst_ref=dst, send_sem=send, recv_sem=recv,
            device_id=device, device_id_type=MESH,
        )

    def own_copy(side, g):
        return remote(
            lhs.at[g, pl.ds(0, 256)], near.at[lands[side], g], own_send.at[side],
            near_recv.at[lands[side], g], sides[side][1],
        )

    def spectra_step(g, _):
        series_copy(g).wait()
        total = None
        for j in range(4):
            w = g * 8 + 2 * j
            x = jnp.concatenate(
                [xbuf[:, w].reshape(3 * SLOTS, LEN), xbuf[:, w + 1].reshape(3 * SLOTS, LEN)], axis=1
            )
            part = jnp.dot(x, tab[j], preferred_element_type=F32)
            total = part if total is None else total + part
        masked = jnp.where(live[None], total.reshape(3, SLOTS, 256), 0.0)
        spec = masked.reshape(3 * SLOTS, 256).astype(BF16)
        lhs[g, 0:384, :] = spec
        when(has_slow & (jnp.logical_not(middle) | (g < AHEAD)), lambda: own_copy(SLOW, g).start())
        own_copy(FAST, g).start()
        for side in (LEFT, RIGHT):
            when(sides[side][0] & (g < FIRST), lambda side=side: own_copy(side, g).start())
        lhs[g, 384:768, 0:128] = spec[:, 128:256]
        lhs[g, 384:768, 128:256] = -spec[:, 0:128]
        wide = spec[0:256].astype(F32)
        power_ref[...] += jnp.sum((wide * wide).reshape(32, 8, 256), axis=0)
        return 0

    lax.fori_loop(0, GROUPS, spectra_step, 0)

    srow = lax.broadcasted_iota(jnp.int32, (8, 128), 0)
    power = 0.5 * jnp.sum(power_ref[...], keepdims=True)
    count = count_ref[0, 0].astype(F32)
    red_send[0] = jnp.where(srow == 0, jnp.broadcast_to(power, (8, 128)), count)

    def across_copy(d):
        return remote(
            red_send.at[0], a_recv.at[d - 1], a_send_sem.at[d - 1], a_recv_sem.at[d - 1], across(d)
        )

    def z_copy(d):
        return remote(
            red_send.at[1], z_recv.at[d - 1], z_send_sem.at[d - 1], z_recv_sem.at[d - 1], along_z(d)
        )

    for d in range(1, 8):
        across_copy(d).start()

    def reduce_copy(s, n):
        directions, passed = stages[s]
        return remote(
            red_recv.at[s - 1, n] if passed else red_send.at[s + 2], red_recv.at[s, n],
            rsend.at[s, n], rrecv.at[s, n], along_y(directions[n]),
        )

    def reduce_start(s):
        for n in range(len(stages[s][0])):
            reduce_copy(s, n).start()

    def reduce_end(s):
        total = red_send[s + 2]
        for n in range(len(stages[s][0])):
            reduce_copy(s, n).wait()
            total = total + red_recv[s, n]
        red_send[s + 3] = total

    total = red_send[0]
    for d in range(1, 8):
        across_copy(d).wait()
        total = total + a_recv[d - 1]
    red_send[1] = total
    for d in range(1, zs):
        z_copy(d).start()

    @pl.when(middle)
    def _():
        for g in range(AHEAD, GROUPS):
            own_copy(SLOW, g).start()

    for m in range(3):
        total = None
        for g in range(GROUPS):
            part = nt_dot(lhs[g, m * 256:(m + 1) * 256, :], lhs[g, 0:256, :])
            total = part if total is None else total + part
        for a in range(2):
            cross[OWN, a, m * 256:(m + 1) * 256, :] = total[:, a * 128:(a + 1) * 128]
    diagonal = (
        lax.broadcasted_iota(jnp.int32, (SLOTS, SLOTS), 0)
        == lax.broadcasted_iota(jnp.int32, (SLOTS, SLOTS), 1)
    )

    def pick(r, t, a):
        block = cross[OWN, a, r * 384 + t * 128:r * 384 + (t + 1) * 128, :]
        return jnp.sum(jnp.where(diagonal, block, 0.0), axis=0, keepdims=True)

    gxx, gyy, gre, gim = pick(0, 0, 0), pick(0, 1, 1), pick(0, 1, 0), pick(1, 1, 0)
    gram[OWN] = jnp.concatenate([gxx, gyy, gre, gim, gxx, gyy, gre, gim], axis=0)

    def gram_copy(side):
        return remote(
            gram.at[OWN], gram.at[lands[side]], gown_send.at[side], gram_recv.at[lands[side]],
            sides[side][1],
        )

    for side in range(4):
        when(sides[side][0], lambda side=side: gram_copy(side).start())

    forwards = (
        (LEFT, FAST, FAST_LEFT), (RIGHT, FAST, FAST_RIGHT),
        (LEFT, SLOW, SLOW_LEFT), (RIGHT, SLOW, SLOW_RIGHT),
        (SLOW, LEFT, SLOW_RIGHT), (SLOW, RIGHT, SLOW_LEFT),
    )

    def fwd_copy(f, g, n=None):
        source, side, role = forwards[f]
        at = g if n is None else pl.ds(g, n)
        return remote(
            near.at[source, at], near.at[role, at], fwd_send.at[f],
            near_recv.at[role, g], sides[side][1],
        )

    def fwd_gram(f):
        source, side, role = forwards[f]
        return remote(
            gram.at[source], gram.at[role], gfwd_send.at[f], gram_recv.at[role], sides[side][1]
        )

    def arrived(role, g):
        remote(
            near.at[role, g], near.at[role, g], own_send.at[0], near_recv.at[role, g], fast_dev
        ).wait_recv()

    def gram_arrived(role):
        remote(
            gram.at[role], gram.at[role], gown_send.at[0], gram_recv.at[role], fast_dev
        ).wait_recv()

    def accumulate(role, g, n=1):
        for m in range(3):
            total = None
            for k in range(n):
                part = nt_dot(lhs[g + k, m * 256:(m + 1) * 256, :], near[role, g + k])
                total = part if total is None else total + part
            for a in range(2):
                cross[role, a, m * 256:(m + 1) * 256, :] += total[:, a * 128:(a + 1) * 128]

    total = red_send[1]
    for d in range(1, zs):
        z_copy(d).wait()
        total = total + z_recv[d - 1]
    red_send[2] = total
    for g in range(FIRST, AHEAD + FIRST):
        for side in (LEFT, RIGHT):
            when(sides[side][0], lambda side=side, g=g: own_copy(side, g).start())
    if stages:
        reduce_start(0)
    cross[0:8] = jnp.zeros((8, 2, 768, 128), F32)

    fast_base = (2 - 2 * parity) * 3
    slow_base = 2 * parity * 3
    tile_code = {
        OWN: 4, LEFT: 3, RIGHT: 5, FAST: fast_base + 1, SLOW: slow_base + 1,
        FAST_LEFT: fast_base, FAST_RIGHT: fast_base + 2,
        SLOW_LEFT: slow_base, SLOW_RIGHT: slow_base + 2,
    }

    lane = lax.broadcasted_iota(jnp.int32, (8, 128), 1)
    masks = [(lane & (BLOCK * bit)) != 0 for bit in (1, 2, 4)]

    def spread(role, h):
        for a in range(2):
            for t in range(3):
                for r in range(2):
                    for half in range(2):
                        column = ((a * 3 + t) * 2 + r) * 256 + half * 128
                        base = r * 384 + t * 128 + half * 8
                        moved = group_transpose(
                            [cross[role, a, pl.ds(base + i, 8, stride=BLOCK), :] for i in range(8)], masks
                        )
                        for q in range(0, 8, 2):
                            x = jnp.concatenate([moved[q], moved[q + 1]], axis=0)
                            high = x.astype(BF16)
                            low = (x - high.astype(F32)).astype(BF16)
                            at = pl.multiple_of(h * 128 + q * 8, 16)
                            picked[pl.ds(at, 16), column:column + 128] = high
                            at = pl.multiple_of(h * 128 + 64 + q * 8, 16)
                            picked[pl.ds(at, 16), column:column + 128] = low

    def gather(codes, first=None):
        index = lax.broadcasted_iota(jnp.int32, (pairs, 128), 1) % 64
        have = code_ref[...]
        hot = [
            jnp.where(have == (index + c * 64).astype(F32), 1.0, 0.0).astype(BF16) for c in codes
        ]
        hot = jnp.concatenate(hot, axis=1)
        for plane in range(12):
            out_ref[plane] += jnp.dot(
                hot, picked[:, plane * 256:(plane + 1) * 256], preferred_element_type=F32
            )

    def spread_two(first, second, codes):
        def tile(h, _):
            spread(jnp.where(h == 0, first, second), h)
            return 0
        lax.fori_loop(0, 2, tile, 0)
        gather(codes)

    def accumulate_roles(first, count, c, wait):
        def one(k, _):
            role = first + k + 2 * (k // 2)
            here = jnp.where(role % 2 == 0, has_left, has_right)
            if first == SLOW_LEFT:
                here = here & has_slow

            @pl.when(here)
            def _():
                @pl.when(role >= FAST_LEFT)
                def _():
                    arrived(role, c)
                    arrived(role, c + 1)
                accumulate(role, c, 2)
            return 0
        lax.fori_loop(0, count, one, 0)

    out_ref[...] = jnp.zeros(out_ref.shape, F32)

    def step(g, _):
        for s in range(len(stages) - 1):
            @pl.when(g == 7)
            def _(s=s):
                reduce_end(s)
                reduce_start(s + 1)

        @pl.when(has_slow & (g < 4) & jnp.logical_not(special))
        def _():
            for k in range(2):
                arrived(SLOW, 2 * g + k)

        for own_side, f_fast, f_slow, next_special, f_early in (
            (LEFT, 0, 2, left_special, 4), (RIGHT, 1, 3, right_special, 5),
        ):
            def service(own_side=own_side, f_fast=f_fast, f_slow=f_slow, next_special=next_special, f_early=f_early):
                when(g + AHEAD + FIRST < GROUPS, lambda: own_copy(own_side, g + AHEAD + FIRST).start())
                late = g + AHEAD + FIRST - GROUPS
                when(has_slow & (late >= 0) & (late < EARLY) & jnp.logical_not(special | next_special),
                     lambda: fwd_copy(f_early, late).start())
                arrived(own_side, g)
                when(has_slow & ((g >= EARLY) | next_special) & jnp.logical_not(special),
                     lambda: fwd_copy(f_slow, g).start())
                fwd_copy(f_fast, g).start()
            when(sides[own_side][0], service)

        @pl.when((left_special | right_special) & (g >= 4))
        def _():
            for k in range(2):
                c = 2 * (g - 4) + k
                when(left_special, lambda: fwd_copy(4, c).start())
                when(right_special, lambda: fwd_copy(5, c).start())

        @pl.when(g == GROUPS - 3)
        def _():
            for role, here in ((LEFT, has_left), (RIGHT, has_right)):
                when(here, lambda role=role: gram_arrived(role))
            for f in range(4):
                source, side, _ = forwards[f]
                when(both(sides[source][0], sides[side][0]), lambda f=f: fwd_gram(f).start())

        @pl.when(g % 2 == 1)
        def _():
            accumulate_roles(LEFT, 4, g - 1, True)

        @pl.when(g == 2)
        def _():
            for k in range(GROUPS):
                arrived(FAST, k)

        @pl.when((g == 2) | ((g == 4) & has_slow & jnp.logical_not(special)))
        def _():
            accumulate(jnp.where(g == 2, FAST, SLOW), 0, GROUPS)

        @pl.when((g == 5) | (g == 6))
        def _():
            spread_two(
                jnp.where(g == 5, OWN, slow_now), FAST,
                (jnp.where(g == 5, 4, slow_now_code), jnp.where(g == 5, tile_code[FAST], -5)),
            )

        @pl.when((g == 7) & has_slow & jnp.logical_not(special))
        def _():
            accumulate_roles(SLOW_LEFT, 2, 2, True)
        return 0

    lacks = jnp.where(has_left, SLOW_RIGHT, SLOW_LEFT)
    lacks_code = jnp.where(has_left, tile_code[SLOW_RIGHT], tile_code[SLOW_LEFT])
    slow_now = jnp.where(special, lacks, SLOW)
    slow_now_code = jnp.where(special, lacks_code, tile_code[SLOW])
    lax.fori_loop(0, GROUPS, step, 0)

    def pair_step(k, _):
        @pl.when((k == 1) & has_slow & jnp.logical_not(special))
        def _():
            accumulate_roles(SLOW_LEFT, 2, 4, True)

        @pl.when((k == 2) & has_slow)
        def _():
            def last_step(n, _):
                c = (2 * n + 2) % GROUPS
                accumulate_roles(SLOW_LEFT, 2, c, True)
                return 0
            lax.fori_loop(jnp.where(special, 0, 2), 4, last_step, 0)

            @pl.when(special)
            def _():
                for g in range(GROUPS):
                    arrived(SLOW, g)
                accumulate(SLOW, 0, GROUPS)

        first = jnp.where(k == 0, LEFT, jnp.where(k == 1, FAST_LEFT, SLOW_LEFT))
        code_a = jnp.where(k == 0, 3, jnp.where(k == 1, fast_base, slow_base))
        swap_a = (k == 2) & special & has_right
        swap_b = (k == 2) & special & has_left
        spread_two(
            jnp.where(swap_a, SLOW, first), jnp.where(swap_b, SLOW, first + 1),
            (jnp.where(swap_a, tile_code[SLOW], code_a), jnp.where(swap_b, tile_code[SLOW], code_a + 2)),
        )
        return 0

    lax.fori_loop(0, 3, pair_step, 0)

    if stages:
        reduce_end(len(stages) - 1)
    for role, here in (
        (FAST, None), (SLOW, has_slow), (FAST_LEFT, has_left), (FAST_RIGHT, has_right),
        (SLOW_LEFT, has_slow & has_left), (SLOW_RIGHT, has_slow & has_right),
    ):
        when(here, lambda role=role: gram_arrived(role))

    summed = red_send[len(stages) + 2]
    ridge = summed[0:1, :] / summed[1:2, :] + 1e-06
    upper = gram[:, 0, :] + ridge
    lower = gram[:, 1, :] + ridge
    gre, gim = gram[:, 2, :], gram[:, 3, :]
    inverse = 1.0 / (upper * lower - (gre * gre + gim * gim))
    row8 = lax.broadcasted_iota(jnp.int32, (8, 128), 0)
    own_block = row8 == lane // BLOCK
    repeat = (
        lax.broadcasted_iota(jnp.int32, (128, 128), 0) % BLOCK
        == lax.broadcasted_iota(jnp.int32, (128, 128), 1) % BLOCK
    ).astype(F32).astype(BF16)

    def split(x):
        high = x.astype(BF16)
        return high, (x - high.astype(F32)).astype(BF16)

    have = code_ref[...]
    blocks = jnp.floor(have * 0.125)
    index = lax.broadcasted_iota(jnp.int32, (pairs, 128), 1)
    order = [tile_code[r] for r in range(9)]
    wanted = jnp.full((1, 128), -5, jnp.int32)
    flat = lax.broadcasted_iota(jnp.int32, (1, 128), 1)
    for r in range(9):
        wanted = jnp.where(flat // 8 == r, order[r] * 8 + flat % 8, wanted)
    hot = jnp.where(blocks == wanted.astype(F32), 1.0, 0.0).astype(BF16)
    for n, value in enumerate((lower, upper, gre, gim)):
        value = value * inverse
        rows = [
            jnp.where(own_block, jnp.broadcast_to(value[r:r + 1], (8, 128)), 0.0) for r in range(9)
        ]
        rows = jnp.concatenate(rows + [jnp.zeros((56, 128), F32)], axis=0)
        high, low = split(rows)
        rows = (
            jnp.dot(high, repeat, preferred_element_type=F32)
            + jnp.dot(low, repeat, preferred_element_type=F32)
        )
        high, low = split(rows)
        coef_ref[n] = (
            jnp.dot(hot, high, preferred_element_type=F32)
            + jnp.dot(hot, low, preferred_element_type=F32)
        )

    def solve_step(e, _):
        at = pl.ds(pl.multiple_of(e * 32, 32), 32)
        lower, upper, gre, gim = coef_ref[0, at, :], coef_ref[1, at, :], coef_ref[2, at, :], coef_ref[3, at, :]
        for t in range(3):
            for half in range(2):
                lanes = slice(half * 128, (half + 1) * 128)
                first_re, first_im = out_ref[2 * t, at, lanes], out_ref[2 * t + 1, at, lanes]
                second_re, second_im = out_ref[6 + 2 * t, at, lanes], out_ref[7 + 2 * t, at, lanes]
                out_ref[2 * t, at, lanes] = lower * first_re - (gre * second_re - gim * second_im)
                out_ref[2 * t + 1, at, lanes] = lower * first_im - (gre * second_im + gim * second_re)
                out_ref[6 + 2 * t, at, lanes] = upper * second_re - (gre * first_re + gim * first_im)
                out_ref[7 + 2 * t, at, lanes] = upper * second_im - (gre * first_im - gim * first_re)
        return 0

    lax.fori_loop(0, pairs // 32, solve_step, 0)

    for side in range(4):
        def done(side=side):
            remote(
                near.at[0], near.at[0], own_send.at[side], near_recv.at[0, 0], fast_dev
            ).wait_send()
            gram_copy(side).wait_send()
        when(sides[side][0], done)
    for f, next_special in enumerate((None, None, left_special, right_special)):
        source, side, _ = forwards[f]

        def done(f=f, side=side, next_special=next_special):
            if side == FAST:
                fwd_copy(f, 0, GROUPS).wait_send()
            else:
                when(jnp.logical_not(special | next_special),
                     lambda: fwd_copy(f, EARLY, GROUPS - EARLY).wait_send())
                when(next_special, lambda: fwd_copy(f, 0, GROUPS).wait_send())
            fwd_gram(f).wait_send()
        when(both(sides[source][0], sides[side][0]), done)
    for f, here, next_special in ((4, has_left, left_special), (5, has_right, right_special)):
        when(has_slow & here & jnp.logical_not(special | next_special),
             lambda f=f: fwd_copy(f, 0, EARLY).wait_send())
        when(next_special, lambda f=f: fwd_copy(f, 0, GROUPS).wait_send())


def per_device(n_lat, n_lon, series, station_count, pair_count, pair_list, band_bins):
    pairs = pair_list.shape[-1]
    smem = pl.BlockSpec(memory_space=pltpu.SMEM)
    vmem = pl.BlockSpec(memory_space=pltpu.VMEM)
    stages = n_lat // 8
    zs = n_lon // 2
    dma = pltpu.SemaphoreType.DMA
    solved = pl.pallas_call(
        functools.partial(kernel, n_lat, n_lon, pairs),
        out_shape=pltpu.VMEM((12, pairs, BLOCK * BLOCK), F32),
        in_specs=[smem, smem, smem, vmem, vmem, pl.BlockSpec(memory_space=pl.ANY)],
        out_specs=vmem,
        scratch_shapes=[
            pltpu.VMEM((3, WIN, SLOTS, LEN), BF16),
            pltpu.VMEM((4, 2 * LEN, 256), BF16),
            pltpu.VMEM((8, GROUPS, 256, 256), BF16),
            pltpu.VMEM((GROUPS, 768, 256), BF16),
            pltpu.VMEM((9, 8, 128), F32),
            pltpu.VMEM((8, 256), F32),
            pltpu.VMEM((stages + 3, 8, 128), F32),
            pltpu.VMEM((max(stages, 1), 2, 8, 128), F32),
            pltpu.VMEM((7, 8, 128), F32),
            pltpu.VMEM((zs - 1, 8, 128), F32),
            pltpu.VMEM((9, 2, 768, 128), F32),
            pltpu.VMEM((256, 12 * 256), BF16),
            pltpu.VMEM((pairs, 128), F32),
            pltpu.VMEM((4, pairs, 128), F32),
            dma((GROUPS,)),
            dma((8, GROUPS)),
            dma((4,)),
            dma((6,)),
            dma((8,)),
            dma((4,)),
            dma((4,)),
            dma((max(stages, 1), 2)),
            dma((max(stages, 1), 2)),
            dma((7,)),
            dma((7,)),
            dma((zs - 1,)),
            dma((zs - 1,)),
        ],
        compiler_params=pltpu.CompilerParams(
            collective_id=0, has_side_effects=True, vmem_limit_bytes=56 * 1024 * 1024
        ),
    )(
        station_count,
        pair_count,
        band_bins,
        pair_list.reshape(3, 1, pairs),
        jnp.asarray(dft_matrix()),
        series.reshape(3, WIN, SLOTS, LEN),
    )
    return solved.transpose(1, 0, 2)[None, None]


def solution(mesh):
    in_specs = (
        P("lat", "lon", None, None, None, None),
        P("lat", "lon"),
        P("lat", "lon"),
        P("lat", "lon", None, None),
        P(),
    )
    out_specs = P("lat", "lon", None, None, None)
    return jax.shard_map(
        functools.partial(per_device, mesh.shape["lat"], mesh.shape["lon"]),
        mesh=mesh, in_specs=in_specs, out_specs=out_specs, check_vma=False,
    )
```

```python
import functools
import math

import jax
import jax.numpy as jnp
import ml_dtypes
import numpy as np
from jax import lax
from jax.experimental import pallas as pl
from jax.experimental.pallas import tpu as pltpu
from jax.sharding import PartitionSpec as P

BLOCK = 16
SLOTS = 128
WIN = 64
LEN = 128
NBAND = 16
GROUPS = 8
FIRST = 1
AHEAD = 2
EARLY, EARLY_MIDDLE = 1, 2
F32 = jnp.float32
BF16 = jnp.bfloat16
MESH = pl.DeviceIdType.MESH

LEFT, RIGHT, FAST, SLOW, FAST_LEFT, FAST_RIGHT, SLOW_LEFT, SLOW_RIGHT, OWN = range(9)


def dft_matrix():
    samples = np.arange(LEN)
    bins = np.arange(LEN // 2)
    phase = (samples[:, None] * bins[None]) % LEN
    angle = phase.astype(np.float32) * np.float32(2.0 * math.pi / LEN)
    factor = np.float32(1.0 / math.sqrt(LEN))
    both = np.concatenate([np.cos(angle) * factor, -np.sin(angle) * factor], axis=1)
    return both.astype(ml_dtypes.bfloat16)


def nt_dot(a, b):
    return lax.dot_general(a, b, (((1,), (1,)), ((), ())), preferred_element_type=F32)


def group_transpose(parts, masks):
    def skew(v):
        for bit, mask in zip((1, 2, 4), masks):
            v = [jnp.where(mask, v[(k + bit) % 8], v[k]) for k in range(8)]
        return v

    v = [x if d == 0 else pltpu.roll(x, d * BLOCK, 1) for d, x in enumerate(skew(parts))]
    v = skew(v)
    return [v[(-q) % 8] for q in range(8)]


def kernel(
    n_lat, n_lon, pairs,
    count_ref, pairs_ref, bins_ref, list_ref, dft_ref, series_ref, out_ref,
    xbuf, tab, near, lhs, gram, power_ref, red_send, red_recv, total_ref, z_recv, cross, picked, code_ref, coef_ref,
    series_sem, near_recv, own_send, fwd_send, gram_recv, gown_send, gfwd_send, rsend, rrecv, z_send_sem, z_recv_sem, total_recv,
):
    lat, lon = lax.axis_index("lat"), lax.axis_index("lon")
    parity = lat % 2
    fast_lat = lat + 1 - 2 * parity
    slow_lat = lat - 1 + 2 * parity
    has_slow = (slow_lat >= 0) & (slow_lat < n_lat)
    has_left, has_right = lon > 0, lon < n_lon - 1
    middle = (lat == n_lat // 2 - 1) | (lat == n_lat // 2)
    special = middle & ((lon == 0) | (lon == n_lon - 1))
    edge = (lon == 0) | (lon == n_lon - 1)
    early_here = jnp.where(middle, EARLY_MIDDLE, EARLY)
    to_edge = {LEFT: lon == 1, RIGHT: lon == n_lon - 2}
    left_special = middle & (lon == 1)
    right_special = middle & (lon == n_lon - 2)

    left_dev, right_dev = (lat, lon - 1), (lat, lon + 1)
    fast_dev, slow_dev = (fast_lat, lon), (slow_lat, lon)
    sides = {LEFT: (has_left, left_dev), RIGHT: (has_right, right_dev),
             FAST: (None, fast_dev), SLOW: (has_slow, slow_dev)}
    lands = {LEFT: RIGHT, RIGHT: LEFT, FAST: FAST, SLOW: SLOW}

    def when(cond, action):
        if cond is None:
            action()
        else:
            pl.when(cond)(action)

    def both(*conds):
        conds = [c for c in conds if c is not None]
        total = None
        for c in conds:
            total = c if total is None else total & c
        return total

    half_lat, half_lon = n_lat // 2, n_lon // 2
    ys, zs = half_lat // 2, half_lon
    x_hi, y = lat // half_lat, lat % half_lat // 2
    x_lo, z = lon // half_lon, lon % half_lon

    def along_z(d):
        return (lat - parity + (parity + d // zs) % 2, x_lo * half_lon + (z + d % zs) % zs)

    def along_x(d):
        x = (2 * x_hi + x_lo + d + 4) % 4
        return (x // 2 * half_lat + lat % half_lat, x % 2 * half_lon + z)

    def along_y(d):
        return (x_hi * half_lat + (y + d + ys) % ys * 2 + parity, lon)

    stages = [
        (find, (1, -1) if k < (size - 1) // 2 else (1,), k > 0)
        for find, size in ((along_x, 4), (along_y, ys)) for k in range(size // 2)
    ]
    outer = ((z == 0) | (z == zs - 1)) if zs > 2 else z < 0
    inner = jnp.logical_not(outer)
    to_low, to_high = (z == 1) & inner, (z == zs - 2) & inner
    rings = [along_x(1), along_x(-1)] + [along_y(d) for d in ((1, -1) if ys > 1 else ())]
    rings += [along_z(d) for d in range(1, 2 * zs)]

    barrier = pltpu.get_barrier_semaphore()

    def greet(target):
        pl.semaphore_signal(barrier, inc=1, device_id=target, device_id_type=MESH)

    gram[...] = jnp.zeros((9, 8, 128), F32)
    for here, target in sides.values():
        when(here, functools.partial(greet, target))
    for target in rings:
        greet(target)

    def series_copy(g):
        return pltpu.make_async_copy(
            series_ref.at[:, pl.ds(g * 8, 8)], xbuf.at[:, pl.ds(g * 8, 8)], series_sem.at[g]
        )

    for g in range(GROUPS):
        series_copy(g).start()

    lane = lax.broadcasted_iota(jnp.int32, (LEN, 256), 1)
    row = lax.broadcasted_iota(jnp.int32, (LEN, 256), 0)
    bins = jnp.zeros((LEN, 256), jnp.int32)
    for k in range(NBAND):
        bins = jnp.where(lane % NBAND == k, bins_ref[k], bins)
    chosen = (row % 64 == bins) & (row // 64 == lane // 128)
    full = jnp.dot(dft_ref[...], chosen.astype(F32).astype(BF16), preferred_element_type=F32)
    window = (lane // NBAND) % 8
    for j in range(4):
        for h in range(2):
            tab[j, h * LEN:(h + 1) * LEN, :] = jnp.where(window == 2 * j + h, full, 0.0).astype(BF16)
    live = row < count_ref[0, 0]
    power_ref[...] = jnp.zeros((8, 256), F32)

    greeted = (
        has_slow.astype(jnp.int32) + has_left.astype(jnp.int32) + has_right.astype(jnp.int32)
        + (1 + len(rings))
    )
    pl.semaphore_wait(barrier, greeted)

    def remote(src, dst, send, recv, device):
        return pltpu.make_async_remote_copy(
            src_ref=src, dst_ref=dst, send_sem=send, recv_sem=recv,
            device_id=device, device_id_type=MESH,
        )

    def own_copy(side, g):
        return remote(
            lhs.at[g, pl.ds(0, 256)], near.at[lands[side], g], own_send.at[side],
            near_recv.at[lands[side], g], sides[side][1],
        )

    def spectra_step(g, _):
        series_copy(g).wait()
        total = None
        for j in range(4):
            w = g * 8 + 2 * j
            x = jnp.concatenate(
                [xbuf[:, w].reshape(3 * SLOTS, LEN), xbuf[:, w + 1].reshape(3 * SLOTS, LEN)], axis=1
            )
            part = jnp.dot(x, tab[j], preferred_element_type=F32)
            total = part if total is None else total + part
        masked = jnp.where(live[None], total.reshape(3, SLOTS, 256), 0.0)
        spec = masked.reshape(3 * SLOTS, 256).astype(BF16)
        lhs[g, 0:384, :] = spec
        when(has_slow, lambda: own_copy(SLOW, g).start())
        own_copy(FAST, g).start()
        for side in (LEFT, RIGHT):
            when(sides[side][0] & (g < FIRST), lambda side=side: own_copy(side, g).start())
        lhs[g, 384:768, 0:128] = spec[:, 128:256]
        lhs[g, 384:768, 128:256] = -spec[:, 0:128]
        wide = spec[0:256].astype(F32)
        power_ref[...] += jnp.sum((wide * wide).reshape(32, 8, 256), axis=0)
        return 0

    lax.fori_loop(0, GROUPS, spectra_step, 0)

    srow = lax.broadcasted_iota(jnp.int32, (8, 128), 0)
    power = 0.5 * jnp.sum(power_ref[...], keepdims=True)
    count = count_ref[0, 0].astype(F32)
    red_send[0] = jnp.where(srow == 0, jnp.broadcast_to(power, (8, 128)), count)

    def z_copy(d):
        return remote(
            red_send.at[0], z_recv.at[d - 1], z_send_sem.at[d - 1], z_recv_sem.at[d - 1], along_z(d)
        )

    for d in range(1, 2 * zs):
        z_copy(d).start()

    def reduce_copy(s, n):
        find, directions, passed = stages[s]
        return remote(
            red_recv.at[s - 1, n] if passed else red_send.at[s + 1], red_recv.at[s, n],
            rsend.at[s, n], rrecv.at[s, n], find(directions[n]),
        )

    def total_copy(d):
        return remote(
            red_send.at[len(stages) + 1], total_ref, z_send_sem.at[0], total_recv, along_z(d + zs if d < 0 else d)
        )

    def reduce_start(s):
        for n in range(len(stages[s][1])):
            reduce_copy(s, n).start()

    def reduce_end(s):
        total = red_send[s + 1]
        for n in range(len(stages[s][1])):
            reduce_copy(s, n).wait()
            total = total + red_recv[s, n]
        red_send[s + 2] = total

    listing = list_ref[...].astype(F32)
    code = listing[0] * 64.0 + listing[2] * 8.0 + listing[1]
    entry = lax.broadcasted_iota(jnp.int32, (1, pairs), 1)
    code = jnp.where(entry < pairs_ref[0, 0], code, -1.0)
    code_ref[...] = jnp.broadcast_to(code, (128, pairs)).T

    for m in range(3):
        total = None
        for g in range(GROUPS):
            part = nt_dot(lhs[g, m * 256:(m + 1) * 256, :], lhs[g, 0:256, :])
            total = part if total is None else total + part
        for a in range(2):
            cross[OWN, a, m * 256:(m + 1) * 256, :] = total[:, a * 128:(a + 1) * 128]
    diagonal = (
        lax.broadcasted_iota(jnp.int32, (SLOTS, SLOTS), 0)
        == lax.broadcasted_iota(jnp.int32, (SLOTS, SLOTS), 1)
    )

    def pick(r, t, a):
        block = cross[OWN, a, r * 384 + t * 128:r * 384 + (t + 1) * 128, :]
        return jnp.sum(jnp.where(diagonal, block, 0.0), axis=0, keepdims=True)

    gxx, gyy, gre, gim = pick(0, 0, 0), pick(0, 1, 1), pick(0, 1, 0), pick(1, 1, 0)
    gram[OWN] = jnp.concatenate([gxx, gyy, gre, gim, gxx, gyy, gre, gim], axis=0)

    def gram_copy(side):
        return remote(
            gram.at[OWN], gram.at[lands[side]], gown_send.at[side], gram_recv.at[lands[side]],
            sides[side][1],
        )

    for side in range(4):
        when(sides[side][0], lambda side=side: gram_copy(side).start())

    forwards = (
        (LEFT, FAST, FAST_LEFT), (RIGHT, FAST, FAST_RIGHT),
        (LEFT, SLOW, SLOW_LEFT), (RIGHT, SLOW, SLOW_RIGHT),
        (SLOW, LEFT, SLOW_RIGHT), (SLOW, RIGHT, SLOW_LEFT),
    )

    def fwd_copy(f, g, n=None):
        source, side, role = forwards[f]
        at = g if n is None else pl.ds(g, n)
        return remote(
            near.at[source, at], near.at[role, at], fwd_send.at[f],
            near_recv.at[role, g], sides[side][1],
        )

    def fwd_gram(f):
        source, side, role = forwards[f]
        return remote(
            gram.at[source], gram.at[role], gfwd_send.at[f], gram_recv.at[role], sides[side][1]
        )

    def arrived(role, g):
        remote(
            near.at[role, g], near.at[role, g], own_send.at[0], near_recv.at[role, g], fast_dev
        ).wait_recv()

    def gram_arrived(role):
        remote(
            gram.at[role], gram.at[role], gown_send.at[0], gram_recv.at[role], fast_dev
        ).wait_recv()

    def accumulate(role, g, n=1):
        for m in range(3):
            total = None
            for k in range(n):
                part = nt_dot(lhs[g + k, m * 256:(m + 1) * 256, :], near[role, g + k])
                total = part if total is None else total + part
            for a in range(2):
                cross[role, a, m * 256:(m + 1) * 256, :] += total[:, a * 128:(a + 1) * 128]

    total = red_send[0]
    for d in range(1, 2 * zs):
        z_copy(d).wait()
        total = total + z_recv[d - 1]
    red_send[1] = total
    for g in range(FIRST, AHEAD + FIRST):
        for side in (LEFT, RIGHT):
            when(sides[side][0], lambda side=side, g=g: own_copy(side, g).start())
    pl.when(inner)(lambda: reduce_start(0))
    cross[0:8] = jnp.zeros((8, 2, 768, 128), F32)

    fast_base = (2 - 2 * parity) * 3
    slow_base = 2 * parity * 3
    tile_code = {
        OWN: 4, LEFT: 3, RIGHT: 5, FAST: fast_base + 1, SLOW: slow_base + 1,
        FAST_LEFT: fast_base, FAST_RIGHT: fast_base + 2,
        SLOW_LEFT: slow_base, SLOW_RIGHT: slow_base + 2,
    }

    lane = lax.broadcasted_iota(jnp.int32, (8, 128), 1)
    masks = [(lane & (BLOCK * bit)) != 0 for bit in (1, 2, 4)]

    def spread(role, h):
        for a in range(2):
            for t in range(3):
                for r in range(2):
                    for half in range(2):
                        column = ((a * 3 + t) * 2 + r) * 256 + half * 128
                        base = r * 384 + t * 128 + half * 8
                        moved = group_transpose(
                            [cross[role, a, pl.ds(base + i, 8, stride=BLOCK), :] for i in range(8)], masks
                        )
                        for q in range(0, 8, 2):
                            x = jnp.concatenate([moved[q], moved[q + 1]], axis=0)
                            high = x.astype(BF16)
                            low = (x - high.astype(F32)).astype(BF16)
                            at = pl.multiple_of(h * 128 + q * 8, 16)
                            picked[pl.ds(at, 16), column:column + 128] = high
                            at = pl.multiple_of(h * 128 + 64 + q * 8, 16)
                            picked[pl.ds(at, 16), column:column + 128] = low

    def gather(codes, first=None):
        index = lax.broadcasted_iota(jnp.int32, (pairs, 128), 1) % 64
        have = code_ref[...]
        hot = [
            jnp.where(have == (index + c * 64).astype(F32), 1.0, 0.0).astype(BF16) for c in codes
        ]
        hot = jnp.concatenate(hot, axis=1)
        for plane in range(12):
            out_ref[plane] += jnp.dot(
                hot, picked[:, plane * 256:(plane + 1) * 256], preferred_element_type=F32
            )

    def spread_two(first, second, codes):
        def tile(h, _):
            spread(jnp.where(h == 0, first, second), h)
            return 0
        lax.fori_loop(0, 2, tile, 0)
        gather(codes)

    def accumulate_roles(first, count, c, wait):
        def one(k, _):
            role = first + k + 2 * (k // 2)
            here = jnp.where(role % 2 == 0, has_left, has_right)
            if first == SLOW_LEFT:
                here = here & has_slow

            @pl.when(here)
            def _():
                @pl.when(role >= FAST_LEFT)
                def _():
                    arrived(role, c)
                    arrived(role, c + 1)
                accumulate(role, c, 2)
            return 0
        lax.fori_loop(0, count, one, 0)

    out_ref[...] = jnp.zeros(out_ref.shape, F32)

    def step(g, _):
        for s in range(len(stages)):
            @pl.when((g == 1 + 2 * s) & inner)
            def _(s=s):
                reduce_end(s)
                if s + 1 < len(stages):
                    reduce_start(s + 1)
                else:
                    for here, d in ((to_low, -1), (to_high, 1)):
                        when(here, lambda d=d: total_copy(d).start())

        @pl.when(has_slow & (g == 4) & jnp.logical_not(special))
        def _():
            for k in range(GROUPS):
                arrived(SLOW, k)

        for own_side, f_fast, f_slow, next_special, f_early in (
            (LEFT, 0, 2, left_special, 4), (RIGHT, 1, 3, right_special, 5),
        ):
            def service(own_side=own_side, f_fast=f_fast, f_slow=f_slow, next_special=next_special, f_early=f_early):
                when(g + AHEAD + FIRST < GROUPS, lambda: own_copy(own_side, g + AHEAD + FIRST).start())
                late = g + AHEAD + FIRST - GROUPS
                when(has_slow & (late >= 0) & (late < early_here) & jnp.logical_not(special | to_edge[own_side]),
                     lambda: fwd_copy(f_early, late).start())
                arrived(own_side, g)
                when(has_slow & (((g >= early_here) | next_special | edge) & jnp.logical_not(special)),
                     lambda: fwd_copy(f_slow, g).start())
                fwd_copy(f_fast, g).start()
            when(sides[own_side][0], service)

        @pl.when((left_special | right_special) & (g >= 4))
        def _():
            for k in range(2):
                c = 2 * (g - 4) + k
                when(left_special, lambda: fwd_copy(4, c).start())
                when(right_special, lambda: fwd_copy(5, c).start())

        @pl.when(g == GROUPS - 3)
        def _():
            for role, here in ((LEFT, has_left), (RIGHT, has_right)):
                when(here, lambda role=role: gram_arrived(role))
            for f in range(4):
                source, side, _ = forwards[f]
                when(both(sides[source][0], sides[side][0]), lambda f=f: fwd_gram(f).start())

        @pl.when(g % 2 == 1)
        def _():
            accumulate_roles(LEFT, 4, g - 1, True)

        @pl.when(g == 2)
        def _():
            for k in range(GROUPS):
                arrived(FAST, k)

        @pl.when((g == 2) | ((g == 4) & has_slow & jnp.logical_not(special)))
        def _():
            accumulate(jnp.where(g == 2, FAST, SLOW), 0, GROUPS)

        @pl.when((g == 5) | (g == 6))
        def _():
            spread_two(
                jnp.where(g == 5, OWN, slow_now), FAST,
                (jnp.where(g == 5, 4, slow_now_code), jnp.where(g == 5, tile_code[FAST], -5)),
            )

        @pl.when((g >= 6) & has_slow & jnp.logical_not(special))
        def _():
            accumulate_roles(SLOW_LEFT, 2, 2 * g - 10, True)
        return 0

    lacks = jnp.where(has_left, SLOW_RIGHT, SLOW_LEFT)
    lacks_code = jnp.where(has_left, tile_code[SLOW_RIGHT], tile_code[SLOW_LEFT])
    slow_now = jnp.where(special, lacks, SLOW)
    slow_now_code = jnp.where(special, lacks_code, tile_code[SLOW])
    lax.fori_loop(0, GROUPS, step, 0)

    def pair_step(k, _):
        @pl.when((k == 1) & has_slow & jnp.logical_not(special))
        def _():
            accumulate_roles(SLOW_LEFT, 2, 6, True)

        @pl.when((k == 2) & has_slow)
        def _():
            def last_step(n, _):
                accumulate_roles(SLOW_LEFT, 2, (2 * n + 2) % GROUPS, True)
                return 0
            lax.fori_loop(jnp.where(special, 0, 3), 4, last_step, 0)

            @pl.when(special)
            def _():
                for g in range(GROUPS):
                    arrived(SLOW, g)
                accumulate(SLOW, 0, GROUPS)

        first = jnp.where(k == 0, LEFT, jnp.where(k == 1, FAST_LEFT, SLOW_LEFT))
        code_a = jnp.where(k == 0, 3, jnp.where(k == 1, fast_base, slow_base))
        swap_a = (k == 2) & special & has_right
        swap_b = (k == 2) & special & has_left
        spread_two(
            jnp.where(swap_a, SLOW, first), jnp.where(swap_b, SLOW, first + 1),
            (jnp.where(swap_a, tile_code[SLOW], code_a), jnp.where(swap_b, tile_code[SLOW], code_a + 2)),
        )
        return 0

    lax.fori_loop(0, 2, pair_step, 0)
    pl.when(outer)(lambda: total_copy(1).wait_recv())
    for here, d in ((to_low, -1), (to_high, 1)):
        when(here, lambda d=d: total_copy(d).wait_send())
    for role, here in (
        (FAST, None), (SLOW, has_slow), (FAST_LEFT, has_left), (FAST_RIGHT, has_right),
        (SLOW_LEFT, has_slow & has_left), (SLOW_RIGHT, has_slow & has_right),
    ):
        when(here, lambda role=role: gram_arrived(role))

    summed = jnp.where(outer, total_ref[...], red_send[len(stages) + 1])
    ridge = summed[0:1, :] / summed[1:2, :] + 1e-06
    upper = gram[:, 0, :] + ridge
    lower = gram[:, 1, :] + ridge
    gre, gim = gram[:, 2, :], gram[:, 3, :]
    inverse = 1.0 / (upper * lower - (gre * gre + gim * gim))
    row8 = lax.broadcasted_iota(jnp.int32, (8, 128), 0)
    own_block = row8 == lane // BLOCK
    repeat = (
        lax.broadcasted_iota(jnp.int32, (128, 128), 0) % BLOCK
        == lax.broadcasted_iota(jnp.int32, (128, 128), 1) % BLOCK
    ).astype(F32).astype(BF16)

    def split(x):
        high = x.astype(BF16)
        return high, (x - high.astype(F32)).astype(BF16)

    have = code_ref[...]
    blocks = jnp.floor(have * 0.125)
    index = lax.broadcasted_iota(jnp.int32, (pairs, 128), 1)
    order = [tile_code[r] for r in range(9)]
    wanted = jnp.full((1, 128), -5, jnp.int32)
    flat = lax.broadcasted_iota(jnp.int32, (1, 128), 1)
    for r in range(9):
        wanted = jnp.where(flat // 8 == r, order[r] * 8 + flat % 8, wanted)
    hot = jnp.where(blocks == wanted.astype(F32), 1.0, 0.0).astype(BF16)
    for n, value in enumerate((lower, upper, gre, gim)):
        value = value * inverse
        rows = [
            jnp.where(own_block, jnp.broadcast_to(value[r:r + 1], (8, 128)), 0.0) for r in range(9)
        ]
        rows = jnp.concatenate(rows + [jnp.zeros((56, 128), F32)], axis=0)
        high, low = split(rows)
        rows = (
            jnp.dot(high, repeat, preferred_element_type=F32)
            + jnp.dot(low, repeat, preferred_element_type=F32)
        )
        high, low = split(rows)
        coef_ref[n] = (
            jnp.dot(hot, high, preferred_element_type=F32)
            + jnp.dot(hot, low, preferred_element_type=F32)
        )

    lax.fori_loop(2, 3, pair_step, 0)

    def solve_step(e, _):
        at = pl.ds(pl.multiple_of(e * 32, 32), 32)
        lower, upper, gre, gim = coef_ref[0, at, :], coef_ref[1, at, :], coef_ref[2, at, :], coef_ref[3, at, :]
        for t in range(3):
            for half in range(2):
                lanes = slice(half * 128, (half + 1) * 128)
                first_re, first_im = out_ref[2 * t, at, lanes], out_ref[2 * t + 1, at, lanes]
                second_re, second_im = out_ref[6 + 2 * t, at, lanes], out_ref[7 + 2 * t, at, lanes]
                out_ref[2 * t, at, lanes] = lower * first_re - (gre * second_re - gim * second_im)
                out_ref[2 * t + 1, at, lanes] = lower * first_im - (gre * second_im + gim * second_re)
                out_ref[6 + 2 * t, at, lanes] = upper * second_re - (gre * first_re + gim * first_im)
                out_ref[7 + 2 * t, at, lanes] = upper * second_im - (gre * first_im - gim * first_re)
        return 0

    lax.fori_loop(0, pairs // 32, solve_step, 0)

    for side in range(4):
        def done(side=side):
            remote(
                near.at[0], near.at[0], own_send.at[side], near_recv.at[0, 0], fast_dev
            ).wait_send()
            gram_copy(side).wait_send()
        when(sides[side][0], done)
    for f, next_special in enumerate((None, None, left_special, right_special)):
        source, side, _ = forwards[f]

        def done(f=f, side=side, next_special=next_special):
            if side == FAST:
                fwd_copy(f, 0, GROUPS).wait_send()
            else:
                for n, here in ((EARLY, jnp.logical_not(middle)), (EARLY_MIDDLE, middle)):
                    when(here & jnp.logical_not(edge | next_special),
                         lambda n=n: fwd_copy(f, n, GROUPS - n).wait_send())
                when((edge | next_special) & jnp.logical_not(special),
                     lambda: fwd_copy(f, 0, GROUPS).wait_send())
            fwd_gram(f).wait_send()
        when(both(sides[source][0], sides[side][0]), done)
    for f, here, next_special in ((4, has_left, left_special), (5, has_right, right_special)):
        for n, row in ((EARLY, jnp.logical_not(middle)), (EARLY_MIDDLE, middle)):
            when(has_slow & here & row & jnp.logical_not(special | to_edge[forwards[f][1]]),
                 lambda f=f, n=n: fwd_copy(f, 0, n).wait_send())
        when(next_special, lambda f=f: fwd_copy(f, 0, GROUPS).wait_send())


def per_device(n_lat, n_lon, series, station_count, pair_count, pair_list, band_bins):
    pairs = pair_list.shape[-1]
    smem = pl.BlockSpec(memory_space=pltpu.SMEM)
    vmem = pl.BlockSpec(memory_space=pltpu.VMEM)
    stages = 2 + n_lat // 8
    zs = n_lon // 2
    dma = pltpu.SemaphoreType.DMA
    solved = pl.pallas_call(
        functools.partial(kernel, n_lat, n_lon, pairs),
        out_shape=pltpu.VMEM((12, pairs, BLOCK * BLOCK), F32),
        in_specs=[smem, smem, smem, vmem, vmem, pl.BlockSpec(memory_space=pl.ANY)],
        out_specs=vmem,
        scratch_shapes=[
            pltpu.VMEM((3, WIN, SLOTS, LEN), BF16),
            pltpu.VMEM((4, 2 * LEN, 256), BF16),
            pltpu.VMEM((8, GROUPS, 256, 256), BF16),
            pltpu.VMEM((GROUPS, 768, 256), BF16),
            pltpu.VMEM((9, 8, 128), F32),
            pltpu.VMEM((8, 256), F32),
            pltpu.VMEM((stages + 2, 8, 128), F32),
            pltpu.VMEM((stages, 2, 8, 128), F32),
            pltpu.VMEM((8, 128), F32),
            pltpu.VMEM((2 * zs - 1, 8, 128), F32),
            pltpu.VMEM((9, 2, 768, 128), F32),
            pltpu.VMEM((256, 12 * 256), BF16),
            pltpu.VMEM((pairs, 128), F32),
            pltpu.VMEM((4, pairs, 128), F32),
            dma((GROUPS,)),
            dma((8, GROUPS)),
            dma((4,)),
            dma((6,)),
            dma((8,)),
            dma((4,)),
            dma((4,)),
            dma((stages, 2)),
            dma((stages, 2)),
            dma((2 * zs - 1,)),
            dma((2 * zs - 1,)),
            dma,
        ],
        compiler_params=pltpu.CompilerParams(
            collective_id=0, has_side_effects=True, vmem_limit_bytes=56 * 1024 * 1024
        ),
    )(
        station_count,
        pair_count,
        band_bins,
        pair_list.reshape(3, 1, pairs),
        jnp.asarray(dft_matrix()),
        series.reshape(3, WIN, SLOTS, LEN),
    )
    return solved.transpose(1, 0, 2)[None, None]


def solution(mesh):
    in_specs = (
        P("lat", "lon", None, None, None, None),
        P("lat", "lon"),
        P("lat", "lon"),
        P("lat", "lon", None, None),
        P(),
    )
    out_specs = P("lat", "lon", None, None, None)
    return jax.shard_map(
        functools.partial(per_device, mesh.shape["lat"], mesh.shape["lon"]),
        mesh=mesh, in_specs=in_specs, out_specs=out_specs, check_vma=False,
    )
```

```python
import functools
import math

import jax
import jax.numpy as jnp
import ml_dtypes
import numpy as np
from jax import lax
from jax.experimental import pallas as pl
from jax.experimental.pallas import tpu as pltpu
from jax.sharding import PartitionSpec as P

BLOCK = 16
SLOTS = 128
WIN = 64
LEN = 128
NBAND = 16
GROUPS = 8
FIRST = 1
AHEAD = 2
EARLY, EARLY_MIDDLE = 1, 2
F32 = jnp.float32
BF16 = jnp.bfloat16
MESH = pl.DeviceIdType.MESH

LEFT, RIGHT, FAST, SLOW, FAST_LEFT, FAST_RIGHT, SLOW_LEFT, SLOW_RIGHT, OWN = range(9)


def dft_matrix():
    samples = np.arange(LEN)
    bins = np.arange(LEN // 2)
    phase = (samples[:, None] * bins[None]) % LEN
    angle = phase.astype(np.float32) * np.float32(2.0 * math.pi / LEN)
    factor = np.float32(1.0 / math.sqrt(LEN))
    both = np.concatenate([np.cos(angle) * factor, -np.sin(angle) * factor], axis=1)
    return both.astype(ml_dtypes.bfloat16)


def nt_dot(a, b):
    return lax.dot_general(a, b, (((1,), (1,)), ((), ())), preferred_element_type=F32)


def group_transpose(parts, masks):
    def skew(v):
        for bit, mask in zip((1, 2, 4), masks):
            v = [jnp.where(mask, v[(k + bit) % 8], v[k]) for k in range(8)]
        return v

    v = [x if d == 0 else pltpu.roll(x, d * BLOCK, 1) for d, x in enumerate(skew(parts))]
    v = skew(v)
    return [v[(-q) % 8] for q in range(8)]


def kernel(
    n_lat, n_lon, pairs,
    count_ref, pairs_ref, bins_ref, list_ref, dft_ref, series_ref, out_ref,
    xbuf, tab, near, lhs, gram, power_ref, red_send, red_recv, total_ref, z_recv, cross, picked, code_ref, coef_ref,
    series_sem, near_recv, own_send, fwd_send, gram_recv, gown_send, gfwd_send, rsend, rrecv, z_send_sem, z_recv_sem, total_recv,
):
    lat, lon = lax.axis_index("lat"), lax.axis_index("lon")
    parity = lat % 2
    fast_lat = lat + 1 - 2 * parity
    slow_lat = lat - 1 + 2 * parity
    has_slow = (slow_lat >= 0) & (slow_lat < n_lat)
    has_left, has_right = lon > 0, lon < n_lon - 1
    middle = (lat == n_lat // 2 - 1) | (lat == n_lat // 2)
    special = middle & ((lon == 0) | (lon == n_lon - 1))
    edge = (lon == 0) | (lon == n_lon - 1)
    early_here = jnp.where(middle, EARLY_MIDDLE, EARLY)
    to_edge = {LEFT: lon == 1, RIGHT: lon == n_lon - 2}
    left_special = middle & (lon == 1)
    right_special = middle & (lon == n_lon - 2)

    left_dev, right_dev = (lat, lon - 1), (lat, lon + 1)
    fast_dev, slow_dev = (fast_lat, lon), (slow_lat, lon)
    sides = {LEFT: (has_left, left_dev), RIGHT: (has_right, right_dev),
             FAST: (None, fast_dev), SLOW: (has_slow, slow_dev)}
    lands = {LEFT: RIGHT, RIGHT: LEFT, FAST: FAST, SLOW: SLOW}

    def when(cond, action):
        if cond is None:
            action()
        else:
            pl.when(cond)(action)

    def both(*conds):
        conds = [c for c in conds if c is not None]
        total = None
        for c in conds:
            total = c if total is None else total & c
        return total

    half_lat, half_lon = n_lat // 2, n_lon // 2
    ys, zs = half_lat // 2, half_lon
    x_hi, y = lat // half_lat, lat % half_lat // 2
    x_lo, z = lon // half_lon, lon % half_lon

    def along_z(d):
        return (lat - parity + (parity + d // zs) % 2, x_lo * half_lon + (z + d % zs) % zs)

    def along_x(d):
        x = (2 * x_hi + x_lo + d + 4) % 4
        return (x // 2 * half_lat + lat % half_lat, x % 2 * half_lon + z)

    def along_y(d):
        return (x_hi * half_lat + (y + d + ys) % ys * 2 + parity, lon)

    stages = [
        (find, (1, -1) if k < (size - 1) // 2 else (1,), k > 0)
        for find, size in ((along_x, 4), (along_y, ys)) for k in range(size // 2)
    ]
    outer = ((z == 0) | (z == zs - 1)) if zs > 2 else z < 0
    inner = jnp.logical_not(outer)
    to_low, to_high = (z == 1) & inner, (z == zs - 2) & inner
    rings = [along_x(1), along_x(-1)] + [along_y(d) for d in ((1, -1) if ys > 1 else ())]
    rings += [along_z(d) for d in range(1, 2 * zs)]

    barrier = pltpu.get_barrier_semaphore()

    def greet(target):
        pl.semaphore_signal(barrier, inc=1, device_id=target, device_id_type=MESH)

    gram[...] = jnp.zeros((9, 8, 128), F32)
    for here, target in sides.values():
        when(here, functools.partial(greet, target))
    for target in rings:
        greet(target)

    def series_copy(g):
        return pltpu.make_async_copy(
            series_ref.at[:, pl.ds(g * 8, 8)], xbuf.at[:, pl.ds(g * 8, 8)], series_sem.at[g]
        )

    for g in range(GROUPS):
        series_copy(g).start()

    lane = lax.broadcasted_iota(jnp.int32, (LEN, 256), 1)
    row = lax.broadcasted_iota(jnp.int32, (LEN, 256), 0)
    bins = jnp.zeros((LEN, 256), jnp.int32)
    for k in range(NBAND):
        bins = jnp.where(lane % NBAND == k, bins_ref[k], bins)
    chosen = (row % 64 == bins) & (row // 64 == lane // 128)
    full = jnp.dot(dft_ref[...], chosen.astype(F32).astype(BF16), preferred_element_type=F32)
    window = (lane // NBAND) % 8
    for j in range(4):
        for h in range(2):
            tab[j, h * LEN:(h + 1) * LEN, :] = jnp.where(window == 2 * j + h, full, 0.0).astype(BF16)
    live = row < count_ref[0, 0]
    power_ref[...] = jnp.zeros((8, 256), F32)

    greeted = (
        has_slow.astype(jnp.int32) + has_left.astype(jnp.int32) + has_right.astype(jnp.int32)
        + (1 + len(rings))
    )

    def remote(src, dst, send, recv, device):
        return pltpu.make_async_remote_copy(
            src_ref=src, dst_ref=dst, send_sem=send, recv_sem=recv,
            device_id=device, device_id_type=MESH,
        )

    def own_copy(side, g):
        return remote(
            lhs.at[g, pl.ds(0, 256)], near.at[lands[side], g], own_send.at[side],
            near_recv.at[lands[side], g], sides[side][1],
        )

    def send_own(g):
        when(has_slow, lambda: own_copy(SLOW, g).start())
        own_copy(FAST, g).start()
        for side in (LEFT, RIGHT):
            when(sides[side][0] & (g < FIRST), lambda side=side: own_copy(side, g).start())

    def spectra_step(g, first=False):
        series_copy(g).wait()
        total = None
        for j in range(4):
            w = g * 8 + 2 * j
            x = jnp.concatenate(
                [xbuf[:, w].reshape(3 * SLOTS, LEN), xbuf[:, w + 1].reshape(3 * SLOTS, LEN)], axis=1
            )
            part = jnp.dot(x, tab[j], preferred_element_type=F32)
            total = part if total is None else total + part
        masked = jnp.where(live[None], total.reshape(3, SLOTS, 256), 0.0)
        spec = masked.reshape(3 * SLOTS, 256).astype(BF16)
        lhs[g, 0:384, :] = spec
        if first:
            pl.semaphore_wait(barrier, greeted)
        send_own(g)
        lhs[g, 384:768, 0:128] = spec[:, 128:256]
        lhs[g, 384:768, 128:256] = -spec[:, 0:128]
        wide = spec[0:256].astype(F32)
        power_ref[...] += jnp.sum((wide * wide).reshape(32, 8, 256), axis=0)

    spectra_step(0, True)

    def later_spectra(g, _):
        spectra_step(g)
        return 0

    lax.fori_loop(1, GROUPS, later_spectra, 0)

    srow = lax.broadcasted_iota(jnp.int32, (8, 128), 0)
    power = 0.5 * jnp.sum(power_ref[...], keepdims=True)
    count = count_ref[0, 0].astype(F32)
    red_send[0] = jnp.where(srow == 0, jnp.broadcast_to(power, (8, 128)), count)

    def z_copy(d):
        return remote(
            red_send.at[0], z_recv.at[d - 1], z_send_sem.at[d - 1], z_recv_sem.at[d - 1], along_z(d)
        )

    for d in range(1, 2 * zs):
        z_copy(d).start()

    def reduce_copy(s, n):
        find, directions, passed = stages[s]
        return remote(
            red_recv.at[s - 1, n] if passed else red_send.at[s + 1], red_recv.at[s, n],
            rsend.at[s, n], rrecv.at[s, n], find(directions[n]),
        )

    def total_copy(d):
        return remote(
            red_send.at[len(stages) + 1], total_ref, z_send_sem.at[0], total_recv, along_z(d + zs if d < 0 else d)
        )

    def reduce_start(s):
        for n in range(len(stages[s][1])):
            reduce_copy(s, n).start()

    def reduce_end(s):
        total = red_send[s + 1]
        for n in range(len(stages[s][1])):
            reduce_copy(s, n).wait()
            total = total + red_recv[s, n]
        red_send[s + 2] = total

    listing = list_ref[...].astype(F32)
    code = listing[0] * 64.0 + listing[2] * 8.0 + listing[1]
    entry = lax.broadcasted_iota(jnp.int32, (1, pairs), 1)
    code = jnp.where(entry < pairs_ref[0, 0], code, -1.0)
    code_ref[...] = jnp.broadcast_to(code, (128, pairs)).T

    for m in range(3):
        total = None
        for g in range(GROUPS):
            part = nt_dot(lhs[g, m * 256:(m + 1) * 256, :], lhs[g, 0:256, :])
            total = part if total is None else total + part
        for a in range(2):
            cross[OWN, a, m * 256:(m + 1) * 256, :] = total[:, a * 128:(a + 1) * 128]
    diagonal = (
        lax.broadcasted_iota(jnp.int32, (SLOTS, SLOTS), 0)
        == lax.broadcasted_iota(jnp.int32, (SLOTS, SLOTS), 1)
    )

    def pick(r, t, a):
        block = cross[OWN, a, r * 384 + t * 128:r * 384 + (t + 1) * 128, :]
        return jnp.sum(jnp.where(diagonal, block, 0.0), axis=0, keepdims=True)

    gxx, gyy, gre, gim = pick(0, 0, 0), pick(0, 1, 1), pick(0, 1, 0), pick(1, 1, 0)
    gram[OWN] = jnp.concatenate([gxx, gyy, gre, gim, gxx, gyy, gre, gim], axis=0)

    def gram_copy(side):
        return remote(
            gram.at[OWN], gram.at[lands[side]], gown_send.at[side], gram_recv.at[lands[side]],
            sides[side][1],
        )

    for side in range(4):
        when(sides[side][0], lambda side=side: gram_copy(side).start())

    forwards = (
        (LEFT, FAST, FAST_LEFT), (RIGHT, FAST, FAST_RIGHT),
        (LEFT, SLOW, SLOW_LEFT), (RIGHT, SLOW, SLOW_RIGHT),
        (SLOW, LEFT, SLOW_RIGHT), (SLOW, RIGHT, SLOW_LEFT),
    )

    def fwd_copy(f, g, n=None):
        source, side, role = forwards[f]
        at = g if n is None else pl.ds(g, n)
        return remote(
            near.at[source, at], near.at[role, at], fwd_send.at[f],
            near_recv.at[role, g], sides[side][1],
        )

    def fwd_gram(f):
        source, side, role = forwards[f]
        return remote(
            gram.at[source], gram.at[role], gfwd_send.at[f], gram_recv.at[role], sides[side][1]
        )

    def arrived(role, g):
        remote(
            near.at[role, g], near.at[role, g], own_send.at[0], near_recv.at[role, g], fast_dev
        ).wait_recv()

    def gram_arrived(role):
        remote(
            gram.at[role], gram.at[role], gown_send.at[0], gram_recv.at[role], fast_dev
        ).wait_recv()

    def accumulate(role, g, n=1):
        for m in range(3):
            total = None
            for k in range(n):
                part = nt_dot(lhs[g + k, m * 256:(m + 1) * 256, :], near[role, g + k])
                total = part if total is None else total + part
            for a in range(2):
                cross[role, a, m * 256:(m + 1) * 256, :] += total[:, a * 128:(a + 1) * 128]

    total = red_send[0]
    for d in range(1, 2 * zs):
        z_copy(d).wait()
        total = total + z_recv[d - 1]
    red_send[1] = total
    for g in range(FIRST, AHEAD + FIRST):
        for side in (LEFT, RIGHT):
            when(sides[side][0], lambda side=side, g=g: own_copy(side, g).start())
    pl.when(inner)(lambda: reduce_start(0))
    cross[0:8] = jnp.zeros((8, 2, 768, 128), F32)

    fast_base = (2 - 2 * parity) * 3
    slow_base = 2 * parity * 3
    tile_code = {
        OWN: 4, LEFT: 3, RIGHT: 5, FAST: fast_base + 1, SLOW: slow_base + 1,
        FAST_LEFT: fast_base, FAST_RIGHT: fast_base + 2,
        SLOW_LEFT: slow_base, SLOW_RIGHT: slow_base + 2,
    }

    lane = lax.broadcasted_iota(jnp.int32, (8, 128), 1)
    masks = [(lane & (BLOCK * bit)) != 0 for bit in (1, 2, 4)]

    def spread(role, h):
        for a in range(2):
            for t in range(3):
                for r in range(2):
                    for half in range(2):
                        column = ((a * 3 + t) * 2 + r) * 256 + half * 128
                        base = r * 384 + t * 128 + half * 8
                        moved = group_transpose(
                            [cross[role, a, pl.ds(base + i, 8, stride=BLOCK), :] for i in range(8)], masks
                        )
                        for q in range(0, 8, 2):
                            x = jnp.concatenate([moved[q], moved[q + 1]], axis=0)
                            high = x.astype(BF16)
                            low = (x - high.astype(F32)).astype(BF16)
                            at = pl.multiple_of(h * 128 + q * 8, 16)
                            picked[pl.ds(at, 16), column:column + 128] = high
                            at = pl.multiple_of(h * 128 + 64 + q * 8, 16)
                            picked[pl.ds(at, 16), column:column + 128] = low

    def gather(codes, first=None):
        index = lax.broadcasted_iota(jnp.int32, (pairs, 128), 1) % 64
        have = code_ref[...]
        hot = [
            jnp.where(have == (index + c * 64).astype(F32), 1.0, 0.0).astype(BF16) for c in codes
        ]
        hot = jnp.concatenate(hot, axis=1)
        for plane in range(12):
            out_ref[plane] += jnp.dot(
                hot, picked[:, plane * 256:(plane + 1) * 256], preferred_element_type=F32
            )

    def spread_two(first, second, codes):
        def tile(h, _):
            spread(jnp.where(h == 0, first, second), h)
            return 0
        lax.fori_loop(0, 2, tile, 0)
        gather(codes)

    def accumulate_roles(first, count, c, wait):
        def one(k, _):
            role = first + k + 2 * (k // 2)
            here = jnp.where(role % 2 == 0, has_left, has_right)
            if first == SLOW_LEFT:
                here = here & has_slow

            @pl.when(here)
            def _():
                @pl.when(role >= FAST_LEFT)
                def _():
                    arrived(role, c)
                    arrived(role, c + 1)
                accumulate(role, c, 2)
            return 0
        lax.fori_loop(0, count, one, 0)

    out_ref[...] = jnp.zeros(out_ref.shape, F32)

    def step(g, _):
        for s in range(len(stages)):
            @pl.when((g == 1 + 2 * s) & inner)
            def _(s=s):
                reduce_end(s)
                if s + 1 < len(stages):
                    reduce_start(s + 1)
                else:
                    for here, d in ((to_low, -1), (to_high, 1)):
                        when(here, lambda d=d: total_copy(d).start())

        @pl.when(has_slow & (g == 4) & jnp.logical_not(special))
        def _():
            for k in range(GROUPS):
                arrived(SLOW, k)

        for own_side, f_fast, f_slow, next_special, f_early in (
            (LEFT, 0, 2, left_special, 4), (RIGHT, 1, 3, right_special, 5),
        ):
            def service(own_side=own_side, f_fast=f_fast, f_slow=f_slow, next_special=next_special, f_early=f_early):
                when(g + AHEAD + FIRST < GROUPS, lambda: own_copy(own_side, g + AHEAD + FIRST).start())
                late = g + AHEAD + FIRST - GROUPS
                when(has_slow & (late >= 0) & (late < early_here) & jnp.logical_not(special | to_edge[own_side]),
                     lambda: fwd_copy(f_early, late).start())
                arrived(own_side, g)
                when(has_slow & (((g >= early_here) | next_special | edge) & jnp.logical_not(special)),
                     lambda: fwd_copy(f_slow, g).start())
                fwd_copy(f_fast, g).start()
            when(sides[own_side][0], service)

        @pl.when((left_special | right_special) & (g >= 4))
        def _():
            for k in range(2):
                c = 2 * (g - 4) + k
                when(left_special, lambda: fwd_copy(4, c).start())
                when(right_special, lambda: fwd_copy(5, c).start())

        @pl.when(g == GROUPS - 3)
        def _():
            for role, here in ((LEFT, has_left), (RIGHT, has_right)):
                when(here, lambda role=role: gram_arrived(role))
            for f in range(4):
                source, side, _ = forwards[f]
                when(both(sides[source][0], sides[side][0]), lambda f=f: fwd_gram(f).start())

        @pl.when(g % 2 == 1)
        def _():
            accumulate_roles(LEFT, 4, g - 1, True)

        @pl.when(g == 2)
        def _():
            for k in range(GROUPS):
                arrived(FAST, k)

        @pl.when((g == 2) | ((g == 4) & has_slow & jnp.logical_not(special)))
        def _():
            accumulate(jnp.where(g == 2, FAST, SLOW), 0, GROUPS)

        @pl.when((g == 5) | (g == 6))
        def _():
            spread_two(
                jnp.where(g == 5, OWN, slow_now), FAST,
                (jnp.where(g == 5, 4, slow_now_code), jnp.where(g == 5, tile_code[FAST], -5)),
            )

        @pl.when((g >= 6) & has_slow & jnp.logical_not(special))
        def _():
            accumulate_roles(SLOW_LEFT, 2, 2 * g - 10, True)
        return 0

    lacks = jnp.where(has_left, SLOW_RIGHT, SLOW_LEFT)
    lacks_code = jnp.where(has_left, tile_code[SLOW_RIGHT], tile_code[SLOW_LEFT])
    slow_now = jnp.where(special, lacks, SLOW)
    slow_now_code = jnp.where(special, lacks_code, tile_code[SLOW])
    lax.fori_loop(0, GROUPS, step, 0)

    def pair_step(k, _):
        @pl.when((k == 1) & has_slow & jnp.logical_not(special))
        def _():
            accumulate_roles(SLOW_LEFT, 2, 6, True)

        @pl.when((k == 2) & has_slow)
        def _():
            def last_step(n, _):
                accumulate_roles(SLOW_LEFT, 2, (2 * n + 2) % GROUPS, True)
                return 0
            lax.fori_loop(jnp.where(special, 0, 3), 4, last_step, 0)

            @pl.when(special)
            def _():
                for g in range(GROUPS):
                    arrived(SLOW, g)
                accumulate(SLOW, 0, GROUPS)

        first = jnp.where(k == 0, LEFT, jnp.where(k == 1, FAST_LEFT, SLOW_LEFT))
        code_a = jnp.where(k == 0, 3, jnp.where(k == 1, fast_base, slow_base))
        swap_a = (k == 2) & special & has_right
        swap_b = (k == 2) & special & has_left
        spread_two(
            jnp.where(swap_a, SLOW, first), jnp.where(swap_b, SLOW, first + 1),
            (jnp.where(swap_a, tile_code[SLOW], code_a), jnp.where(swap_b, tile_code[SLOW], code_a + 2)),
        )
        return 0

    lax.fori_loop(0, 2, pair_step, 0)
    pl.when(outer)(lambda: total_copy(1).wait_recv())
    for here, d in ((to_low, -1), (to_high, 1)):
        when(here, lambda d=d: total_copy(d).wait_send())
    for role, here in (
        (FAST, None), (SLOW, has_slow), (FAST_LEFT, has_left), (FAST_RIGHT, has_right),
        (SLOW_LEFT, has_slow & has_left), (SLOW_RIGHT, has_slow & has_right),
    ):
        when(here, lambda role=role: gram_arrived(role))

    summed = jnp.where(outer, total_ref[...], red_send[len(stages) + 1])
    ridge = summed[0:1, :] / summed[1:2, :] + 1e-06
    upper = gram[:, 0, :] + ridge
    lower = gram[:, 1, :] + ridge
    gre, gim = gram[:, 2, :], gram[:, 3, :]
    inverse = 1.0 / (upper * lower - (gre * gre + gim * gim))
    row8 = lax.broadcasted_iota(jnp.int32, (8, 128), 0)
    own_block = row8 == lane // BLOCK
    repeat = (
        lax.broadcasted_iota(jnp.int32, (128, 128), 0) % BLOCK
        == lax.broadcasted_iota(jnp.int32, (128, 128), 1) % BLOCK
    ).astype(F32).astype(BF16)

    def split(x):
        high = x.astype(BF16)
        return high, (x - high.astype(F32)).astype(BF16)

    have = code_ref[...]
    blocks = jnp.floor(have * 0.125)
    index = lax.broadcasted_iota(jnp.int32, (pairs, 128), 1)
    order = [tile_code[r] for r in range(9)]
    wanted = jnp.full((1, 128), -5, jnp.int32)
    flat = lax.broadcasted_iota(jnp.int32, (1, 128), 1)
    for r in range(9):
        wanted = jnp.where(flat // 8 == r, order[r] * 8 + flat % 8, wanted)
    hot = jnp.where(blocks == wanted.astype(F32), 1.0, 0.0).astype(BF16)
    for n, value in enumerate((lower, upper, gre, gim)):
        value = value * inverse
        rows = [
            jnp.where(own_block, jnp.broadcast_to(value[r:r + 1], (8, 128)), 0.0) for r in range(9)
        ]
        rows = jnp.concatenate(rows + [jnp.zeros((56, 128), F32)], axis=0)
        high, low = split(rows)
        rows = (
            jnp.dot(high, repeat, preferred_element_type=F32)
            + jnp.dot(low, repeat, preferred_element_type=F32)
        )
        high, low = split(rows)
        coef_ref[n] = (
            jnp.dot(hot, high, preferred_element_type=F32)
            + jnp.dot(hot, low, preferred_element_type=F32)
        )

    lax.fori_loop(2, 3, pair_step, 0)

    def solve_step(e, _):
        at = pl.ds(pl.multiple_of(e * 32, 32), 32)
        lower, upper, gre, gim = coef_ref[0, at, :], coef_ref[1, at, :], coef_ref[2, at, :], coef_ref[3, at, :]
        for t in range(3):
            for half in range(2):
                lanes = slice(half * 128, (half + 1) * 128)
                first_re, first_im = out_ref[2 * t, at, lanes], out_ref[2 * t + 1, at, lanes]
                second_re, second_im = out_ref[6 + 2 * t, at, lanes], out_ref[7 + 2 * t, at, lanes]
                out_ref[2 * t, at, lanes] = lower * first_re - (gre * second_re - gim * second_im)
                out_ref[2 * t + 1, at, lanes] = lower * first_im - (gre * second_im + gim * second_re)
                out_ref[6 + 2 * t, at, lanes] = upper * second_re - (gre * first_re + gim * first_im)
                out_ref[7 + 2 * t, at, lanes] = upper * second_im - (gre * first_im - gim * first_re)
        return 0

    lax.fori_loop(0, pairs // 32, solve_step, 0)

    for side in range(4):
        def done(side=side):
            remote(
                near.at[0], near.at[0], own_send.at[side], near_recv.at[0, 0], fast_dev
            ).wait_send()
            gram_copy(side).wait_send()
        when(sides[side][0], done)
    for f, next_special in enumerate((None, None, left_special, right_special)):
        source, side, _ = forwards[f]

        def done(f=f, side=side, next_special=next_special):
            if side == FAST:
                fwd_copy(f, 0, GROUPS).wait_send()
            else:
                for n, here in ((EARLY, jnp.logical_not(middle)), (EARLY_MIDDLE, middle)):
                    when(here & jnp.logical_not(edge | next_special),
                         lambda n=n: fwd_copy(f, n, GROUPS - n).wait_send())
                when((edge | next_special) & jnp.logical_not(special),
                     lambda: fwd_copy(f, 0, GROUPS).wait_send())
            fwd_gram(f).wait_send()
        when(both(sides[source][0], sides[side][0]), done)
    for f, here, next_special in ((4, has_left, left_special), (5, has_right, right_special)):
        for n, row in ((EARLY, jnp.logical_not(middle)), (EARLY_MIDDLE, middle)):
            when(has_slow & here & row & jnp.logical_not(special | to_edge[forwards[f][1]]),
                 lambda f=f, n=n: fwd_copy(f, 0, n).wait_send())
        when(next_special, lambda f=f: fwd_copy(f, 0, GROUPS).wait_send())


def per_device(n_lat, n_lon, series, station_count, pair_count, pair_list, band_bins):
    pairs = pair_list.shape[-1]
    smem = pl.BlockSpec(memory_space=pltpu.SMEM)
    vmem = pl.BlockSpec(memory_space=pltpu.VMEM)
    stages = 2 + n_lat // 8
    zs = n_lon // 2
    dma = pltpu.SemaphoreType.DMA
    solved = pl.pallas_call(
        functools.partial(kernel, n_lat, n_lon, pairs),
        out_shape=pltpu.VMEM((12, pairs, BLOCK * BLOCK), F32),
        in_specs=[smem, smem, smem, vmem, vmem, pl.BlockSpec(memory_space=pl.ANY)],
        out_specs=vmem,
        scratch_shapes=[
            pltpu.VMEM((3, WIN, SLOTS, LEN), BF16),
            pltpu.VMEM((4, 2 * LEN, 256), BF16),
            pltpu.VMEM((8, GROUPS, 256, 256), BF16),
            pltpu.VMEM((GROUPS, 768, 256), BF16),
            pltpu.VMEM((9, 8, 128), F32),
            pltpu.VMEM((8, 256), F32),
            pltpu.VMEM((stages + 2, 8, 128), F32),
            pltpu.VMEM((stages, 2, 8, 128), F32),
            pltpu.VMEM((8, 128), F32),
            pltpu.VMEM((2 * zs - 1, 8, 128), F32),
            pltpu.VMEM((9, 2, 768, 128), F32),
            pltpu.VMEM((256, 12 * 256), BF16),
            pltpu.VMEM((pairs, 128), F32),
            pltpu.VMEM((4, pairs, 128), F32),
            dma((GROUPS,)),
            dma((8, GROUPS)),
            dma((4,)),
            dma((6,)),
            dma((8,)),
            dma((4,)),
            dma((4,)),
            dma((stages, 2)),
            dma((stages, 2)),
            dma((2 * zs - 1,)),
            dma((2 * zs - 1,)),
            dma,
        ],
        compiler_params=pltpu.CompilerParams(
            collective_id=0, has_side_effects=True, vmem_limit_bytes=56 * 1024 * 1024
        ),
    )(
        station_count,
        pair_count,
        band_bins,
        pair_list.reshape(3, 1, pairs),
        jnp.asarray(dft_matrix()),
        series.reshape(3, WIN, SLOTS, LEN),
    )
    return solved.transpose(1, 0, 2)[None, None]


def solution(mesh):
    in_specs = (
        P("lat", "lon", None, None, None, None),
        P("lat", "lon"),
        P("lat", "lon"),
        P("lat", "lon", None, None),
        P(),
    )
    out_specs = P("lat", "lon", None, None, None)
    return jax.shard_map(
        functools.partial(per_device, mesh.shape["lat"], mesh.shape["lon"]),
        mesh=mesh, in_specs=in_specs, out_specs=out_specs, check_vma=False,
    )
```
